512 devices in a mesh: gx: 4 (over x), gy: 4 (over y), gz: 32 (over z, core).
Axes of the slice: x: 4, y: 4, z: 16, core: 2. Of those that a mesh axis runs over, the one named last changes fastest.
Arguments:
- velocity: float32 [3, 16, 16, 256, 512], P(None, 'gx', 'gy', 'gz'), may hold values from -6 to 6
- viscosity: float32 [16, 16, 256, 512], P('gx', 'gy', 'gz'), may hold values from 0.1 to 1
- fibre_coords: float32 [4, 4, 32, 32, 4, 3, 128], P('gx', 'gy', 'gz'), may hold values from -1 to 1
- fibre_elem: int32 [4, 4, 32, 32, 4], P('gx', 'gy', 'gz'), may hold values from 0 to 127
- block_count: int32 [4, 4, 32, 32], P('gx', 'gy', 'gz'), may hold values from 0 to 4, as said below
- fibre_velocity: float32 [4, 4, 32, 32, 4, 3, 128], P('gx', 'gy', 'gz'), may hold values from -6 to 6
Outputs:
- advection: float32 [3, 16, 16, 256, 512], P(None, 'gx', 'gy', 'gz')
- helmholtz: float32 [3, 16, 16, 256, 512], P(None, 'gx', 'gy', 'gz')
- fibre_drag: float32 [4, 4, 32, 32, 4, 3, 128], P('gx', 'gy', 'gz')
The draws below stay inside these ranges and needn't reach their ends.
Inputs may be any that keep to these rules, and one draw needn't show every extreme that they name: `fibre_elem`: local element index a * 4 * 8 + b * 8 + c on the destination device. The first block_count of the 4 slots to a destination are live; each device has a destination with all 4 slots live.
All inputs are finite; a program needn't handle non-finite values.
Results may differ from the reference program's by a relative error of at most 0.0003.
Values sent between devices are 32-bit elements; how exact they have to be, the bound alone decides.
No kernel may reach another device: no remote copies, remote signals or barrier semaphores. Data moves between devices by JAX's collectives and lax.ppermute only.
A program may use at most 128 MiB of HBM per device.

```python
import math
import jax
import jax.numpy as jnp
from jax import lax

POINTS = 512
BLOCK_POINTS = 128
ELEMS_X = 4
ELEMS_Y = 4
ELEMS_Z = 8
PAIR_BLOCKS = 4
GRID_X = 16
GRID_Y = 16
GRID_Z = 256
N_GX = 4
N_GY = 4
N_GZ = 32


def draw_block_count(key, part):
    key = jax.random.fold_in(key, 11)
    first_key, second_key, third_key = jax.random.split(key, 3)
    base_count = jax.random.randint(first_key, (N_GX, N_GY, N_GZ, N_GZ), 0, PAIR_BLOCKS + 1)
    source_cap = jax.random.randint(second_key, (N_GX, N_GY, N_GZ, 1), 1, PAIR_BLOCKS + 1)
    full_target = jax.random.randint(third_key, (N_GX, N_GY, N_GZ, 1), 0, N_GZ)
    destination = lax.broadcasted_iota(jnp.int32, (N_GX, N_GY, N_GZ, N_GZ), 3)
    counted = jnp.where(destination == full_target, PAIR_BLOCKS, jnp.minimum(base_count, source_cap))
    return counted.astype(jnp.int32)


def place_ends(drawn, rng, least, largest):
    longest = drawn.shape.index(max(drawn.shape))
    spots = []
    for shift in (0, 1):
        where = [jax.random.randint(jax.random.fold_in(rng, axis), (), 0, length) for axis, length in enumerate(drawn.shape)]
        where[longest] = (where[longest] + shift) % drawn.shape[longest]
        spots.append(tuple(where))
    return drawn.at[spots[0]].set(least).at[spots[1]].set(largest)


def levels(rng, dims, cuts, low, largest):
    def one(dim, shards_of):
        steps = jax.random.uniform(jax.random.fold_in(jax.random.fold_in(rng, 6), dim), (shards_of,), jnp.float32, low / len(cuts), largest / len(cuts))
        return jnp.repeat(jnp.exp(steps), dims[dim] // shards_of).reshape((-1,) + (1,) * (len(dims) - dim - 1))

    gain = one(*cuts[0])
    for cut in cuts[1:]:
        gain = gain * one(*cut)
    return gain


def noise(own_key, shape, scale, bound, cuts=(), kind=jnp.bfloat16):
    values = scale * jax.random.normal(own_key, shape, jnp.float32)
    if cuts:
        values = values * levels(own_key, shape, cuts, -0.22, 0.18)
    return jnp.clip(values, -bound, bound).astype(kind)


def setup_inputs(seed: int = 0) -> dict:
    keys = jax.random.split(jax.random.key(seed), 7)
    velocity = noise(keys[0], (3, GRID_X, GRID_Y, GRID_Z, POINTS), 1.0, 6.0, ((1, 4), (2, 4), (3, 32)), jnp.float32)
    viscosity = jnp.clip(jnp.exp(math.log(1.0) - 2.3025851 * jax.random.uniform(keys[1], (GRID_X, GRID_Y, GRID_Z, POINTS), jnp.float32) ** levels(keys[1], (GRID_X, GRID_Y, GRID_Z, POINTS), ((0, 4), (1, 4), (2, 32)), -0.2, 0.2)), 0.1, 1.0)
    fibre_coords = jnp.clip(jax.random.uniform(keys[2], (N_GX, N_GY, N_GZ, N_GZ, PAIR_BLOCKS, 3, BLOCK_POINTS), jnp.float32, -1.0, 1.0) * levels(keys[2], (N_GX, N_GY, N_GZ, N_GZ, PAIR_BLOCKS, 3, BLOCK_POINTS), ((0, 4), (1, 4), (2, 32)), -0.4, 0.0), -1.0, 1.0)
    fibre_elem = place_ends(jax.random.randint(keys[3], (N_GX, N_GY, N_GZ, N_GZ, PAIR_BLOCKS), 0, ELEMS_X * ELEMS_Y * ELEMS_Z), jax.random.fold_in(keys[3], 1), 0, (ELEMS_X * ELEMS_Y * ELEMS_Z) - 1).astype(jnp.int32)
    block_count = draw_block_count(jax.random.fold_in(keys[6], 71), 0)
    fibre_velocity = noise(keys[5], (N_GX, N_GY, N_GZ, N_GZ, PAIR_BLOCKS, 3, BLOCK_POINTS), 1.0, 6.0, ((0, 4), (1, 4), (2, 32)), jnp.float32)
    return dict(velocity=velocity, viscosity=viscosity, fibre_coords=fibre_coords, fibre_elem=fibre_elem, block_count=block_count, fibre_velocity=fibre_velocity)


gll_points = (-1.0, -0.8717401485096066, -0.5917001814331423, -0.2092992179024789, 0.2092992179024789, 0.5917001814331423, 0.8717401485096066, 1.0)
gll_weights = (0.03571428571428571, 0.2107042271435061, 0.3411226924835044, 0.4124587946587038, 0.4124587946587038, 0.3411226924835044, 0.2107042271435061, 0.03571428571428571)
helm_shift = 20.0
drag_scale = 0.5

def gll_tables():
    points = list(gll_points)
    number = len(points)
    barycentric = [1.0] * number
    for row in range(number):
        for other in range(number):
            if other != row:
                barycentric[row] = barycentric[row] / (points[row] - points[other])
    derivative = [[0.0] * number for row in range(number)]
    for row in range(number):
        total = 0.0
        for other in range(number):
            if other != row:
                entry = barycentric[other] / barycentric[row] / (points[row] - points[other])
                derivative[row][other] = entry
                total = total + entry
        derivative[row][row] = -total
    transposed = [[derivative[other][row] for other in range(number)] for row in range(number)]
    mass_list = []
    for first in range(number):
        for second in range(number):
            for third in range(number):
                mass_list.append(gll_weights[first] * gll_weights[second] * gll_weights[third])
    return (derivative, transposed, mass_list)

def along(field, matrix, direction):
    field_shape = field.shape
    nodal = field.reshape(field_shape[:-1] + (8, 8, 8))
    if direction == 0:
        result = jnp.einsum('ai,...ijk->...ajk', matrix, nodal, precision=lax.Precision.HIGHEST)
    elif direction == 1:
        result = jnp.einsum('aj,...ijk->...iak', matrix, nodal, precision=lax.Precision.HIGHEST)
    else:
        result = jnp.einsum('ak,...ijk->...ija', matrix, nodal, precision=lax.Precision.HIGHEST)
    return result.reshape(field_shape)

def fluid_terms(velocity, viscosity):
    derivative, transposed, mass_list = gll_tables()
    forward = jnp.asarray(derivative, velocity.dtype)
    backward = jnp.asarray(transposed, velocity.dtype)
    mass_diag = jnp.asarray(mass_list, velocity.dtype)
    weighted = mass_diag * viscosity
    convective = []
    helmholtz = []
    for component in range(3):
        gradient = [along(velocity[component], forward, direction) for direction in range(3)]
        advected = velocity[0] * gradient[0] + velocity[1] * gradient[1] + velocity[2] * gradient[2]
        convective.append(mass_diag * advected)
        stiffness = along(weighted * gradient[0], backward, 0) + along(weighted * gradient[1], backward, 1)
        stiffness = stiffness + along(weighted * gradient[2], backward, 2)
        helmholtz.append(stiffness + helm_shift * mass_diag * velocity[component])
    return jnp.stack(convective + helmholtz)

def fold_axis(field, elem_axis, node_axis):
    moved = jnp.moveaxis(field, (elem_axis, node_axis), (-2, -1))
    leading = moved.shape[:-2]
    blocks = moved.shape[-2]
    interior = moved[..., :7].reshape(leading + (7 * blocks,))
    interior = jnp.concatenate([interior, jnp.zeros(leading + (1,), field.dtype)], -1)
    last_nodes = jnp.concatenate([jnp.zeros(leading + (blocks, 6), field.dtype), moved[..., 7:]], -1)
    last_nodes = last_nodes.reshape(leading + (7 * blocks,))
    last_nodes = jnp.concatenate([jnp.zeros(leading + (1,), field.dtype), last_nodes], -1)
    return jnp.moveaxis(interior + last_nodes, -1, elem_axis)

def unfold_axis(lattice, lattice_axis, node_pos):
    moved = jnp.moveaxis(lattice, lattice_axis, -1)
    blocks = (moved.shape[-1] - 1) // 7
    leading = moved.shape[:-1]
    interior = moved[..., :7 * blocks].reshape(leading + (blocks, 7))
    closing = moved[..., 7::7][..., None]
    nodal = jnp.concatenate([interior, closing], -1)
    return jnp.moveaxis(nodal, (-2, -1), (lattice_axis, node_pos))

def to_lattice(nodal_cube):
    return fold_axis(fold_axis(fold_axis(nodal_cube, 1, 4), 2, 4), 3, 4)

def from_lattice(lattice):
    return unfold_axis(unfold_axis(unfold_axis(lattice, 3, 4), 2, 4), 1, 4)

def lagrange(position):
    columns = []
    for node in range(8):
        value = jnp.ones_like(position)
        for other in range(8):
            if other != node:
                value = value * ((position - gll_points[other]) / (gll_points[node] - gll_points[other]))
        columns.append(value)
    return jnp.stack(columns, -1)

def interpolate(blocks, coords):
    basis_x = lagrange(coords[..., 0, :])
    basis_y = lagrange(coords[..., 1, :])
    basis_z = lagrange(coords[..., 2, :])
    nodal = blocks.reshape(blocks.shape[:-1] + (64, 8))
    section = jnp.einsum('...cqk,...pk->...cqp', nodal, basis_z, precision=lax.Precision.HIGHEST)
    section = section.reshape(section.shape[:-2] + (8, 8, section.shape[-1]))
    section = jnp.einsum('...cijp,...pj->...cip', section, basis_y, precision=lax.Precision.HIGHEST)
    return jnp.einsum('...cip,...pi->...cp', section, basis_x, precision=lax.Precision.HIGHEST)

def drag_of(sampled, own_velocity, counts):
    relative = sampled - own_velocity
    speed_factor = jnp.sqrt(1.0 + lax.optimization_barrier(jnp.sum(relative * relative, axis=-2, keepdims=True)))
    slot_index = lax.broadcasted_iota(jnp.int32, relative.shape[:2], 1)
    live_mask = (slot_index < counts[:, None])[:, :, None, None]
    return jnp.where(live_mask, drag_scale * speed_factor * relative, jnp.zeros_like(relative))

def reference(velocity, viscosity, fibre_coords, fibre_elem, block_count, fibre_velocity):
    local_terms = fluid_terms(velocity, viscosity)
    nodal_cube = local_terms.reshape(local_terms.shape[:-1] + (8, 8, 8))
    assembled = from_lattice(to_lattice(nodal_cube)).reshape(local_terms.shape)
    per_device = velocity.reshape(3, N_GX, ELEMS_X, N_GY, ELEMS_Y, N_GZ, ELEMS_Z, POINTS)
    per_device = per_device.transpose(1, 3, 5, 2, 4, 6, 0, 7)
    per_device = per_device.reshape(N_GX, N_GY, N_GZ, ELEMS_X * ELEMS_Y * ELEMS_Z, 3, POINTS)
    sources = N_GX * N_GY * N_GZ
    coords = fibre_coords.reshape(sources, N_GZ, PAIR_BLOCKS, 3, BLOCK_POINTS)
    idents = fibre_elem.reshape(sources, N_GZ, PAIR_BLOCKS).astype(jnp.int32)
    counts = block_count.reshape(sources, N_GZ).astype(jnp.int32)
    own_velocity = fibre_velocity.reshape(sources, N_GZ, PAIR_BLOCKS, 3, BLOCK_POINTS)
    destination = jnp.arange(N_GZ, dtype=jnp.int32)[:, None]

    def per_source(items):
        source_index, coord_block, ident_block, count_block, own_block = items
        column_x = source_index // (N_GY * N_GZ)
        column_y = source_index // N_GZ % N_GY
        element_table = per_device[column_x, column_y]
        blocks = element_table[destination, ident_block]
        sampled = interpolate(blocks, coord_block)
        return drag_of(sampled, own_block, count_block)
    fibre_drag = lax.map(per_source, (jnp.arange(sources, dtype=jnp.int32), coords, idents, counts, own_velocity))
    return (assembled[:3], assembled[3:], fibre_drag.reshape(fibre_coords.shape))
```

```python
import jax
import jax.numpy as jnp
import numpy as np
from jax import lax
from jax.experimental import pallas as pl
from jax.experimental.pallas import tpu as pltpu
from jax.sharding import PartitionSpec as P

gll_points = (
    -1.0,
    -0.8717401485096066,
    -0.5917001814331423,
    -0.2092992179024789,
    0.2092992179024789,
    0.5917001814331423,
    0.8717401485096066,
    1.0,
)
gll_weights = (
    0.03571428571428571,
    0.2107042271435061,
    0.3411226924835044,
    0.4124587946587038,
    0.4124587946587038,
    0.3411226924835044,
    0.2107042271435061,
    0.03571428571428571,
)
helm_shift = 20.0
drag_scale = 0.5
UNROLL = 8
VMEM_LIMIT = 48 * 1024 * 1024
f32 = jnp.float32
bf16 = jnp.bfloat16


def derivative_table():
    points = list(gll_points)
    barycentric = [1.0] * 8
    for row in range(8):
        for other in range(8):
            if other != row:
                barycentric[row] = barycentric[row] / (points[row] - points[other])
    derivative = np.zeros((8, 8))
    for row in range(8):
        total = 0.0
        for other in range(8):
            if other != row:
                entry = barycentric[other] / barycentric[row] / (points[row] - points[other])
                derivative[row, other] = entry
                total = total + entry
        derivative[row, row] = -total
    return derivative


def operator_tables():
    derivative = derivative_table()
    identity = np.eye(8)
    kron_x = np.kron(np.kron(derivative, identity), identity)
    kron_y = np.kron(np.eye(4), np.kron(derivative, identity))
    kron_z = np.kron(np.eye(32), derivative)
    kron_yz = np.concatenate([kron_y, kron_z], 0)
    weights = np.asarray(gll_weights)
    mass = (weights[:, None, None] * weights[None, :, None] * weights[None, None, :]).reshape(1, 512)
    return (
        kron_x.astype(np.float32),
        kron_yz.astype(np.float32),
        mass.astype(np.float32),
    )


def pick_table(face):
    node = lax.broadcasted_iota(jnp.int32, (512, 128), 0)
    lane = lax.broadcasted_iota(jnp.int32, (512, 128), 1)
    i, j, k = node >> 6, (node >> 3) & 7, node & 7
    edge = 7 * (face % 2)
    if face < 2:
        hit = (j == edge) & (lane == i * 8 + k)
    else:
        hit = (k == edge) & (lane == i * 8 + j)
    return jnp.where(hit, 1.0, 0.0).astype(bf16)


def edge_table(side, place):
    source = lax.broadcasted_iota(jnp.int32, (128, 128), 0)
    lane = lax.broadcasted_iota(jnp.int32, (128, 128), 1)
    target = (source & 64) + 56 * place + ((source >> 3) & 7)
    hit = ((source & 7) == 7 * side) & (lane == target)
    return jnp.where(hit, 1.0, 0.0).astype(bf16)


def basis_table():
    table = np.zeros((8, 8, 128))
    for node in range(8):
        others = [other for other in range(8) if other != node]
        scale = 1.0
        for place, other in enumerate(others):
            table[place, node] = gll_points[other]
            scale = scale / (gll_points[node] - gll_points[other])
        table[7, node] = scale
    return table.astype(np.float32)


def split(x):
    high = x.astype(bf16)
    low = (x - high.astype(f32)).astype(bf16)
    return high, low


def mm(a, b, dims=((1,), (0,))):
    return lax.dot_general(a, b, (dims, ((), ())), preferred_element_type=f32)


def dot3(x, table, side):
    high, low = split(x)
    dims = ((1,), (side,))
    return mm(high, table[0], dims) + mm(high, table[1], dims) + mm(low, table[0], dims)


def pick(x, table):
    high, low = split(x)
    return mm(high, table) + mm(low, table)


def spread(x, table):
    high, low = split(x)
    dims = ((1,), (1,))
    return mm(high, table, dims) + mm(low, table, dims)


def lane_iota(shape):
    return lax.broadcasted_iota(jnp.int32, shape, len(shape) - 1)


def fluid_kernel(vel_in, visc_in, dx_in, dyz_in, mass_in, adv_out, helm_out, xl, xr, yl, yr, zl, zr, flux, adv, helm, vel, visc, dx_ref, dyz_ref, mass_ref, sems):
    pairs = ((vel_in, vel), (dx_in, dx_ref), (dyz_in, dyz_ref), (visc_in, visc), (mass_in, mass_ref))
    loads = [pltpu.make_async_copy(a, b, sems.at[n]) for n, (a, b) in enumerate(pairs)]
    for load in loads:
        load.start()
    loads[0].wait()
    loads[1].wait()
    v = vel[...].reshape(384, 512)
    dx = split(dx_ref[...])
    flux[0] = dot3(v, dx, 1)
    loads[2].wait()
    dyz = split(dyz_ref[...])
    for half in range(2):
        lanes = slice(256 * half, 256 * half + 256)
        g = dot3(v[:, lanes], dyz, 1)
        flux[1, :, lanes] = g[:, :256]
        flux[2, :, lanes] = g[:, 256:]
    loads[3].wait()
    loads[4].wait()
    mass = mass_ref[...]
    weighted = mass * visc[...]
    for c in range(3):
        rows = slice(128 * c, 128 * c + 128)
        total = vel[0] * flux[0, rows] + vel[1] * flux[1, rows] + vel[2] * flux[2, rows]
        adv[c] = mass * total
        for d in range(3):
            flux[d, rows] = weighted * flux[d, rows]
    stiff = dot3(flux[0], dx, 0)
    helm[...] = (stiff + (helm_shift * mass) * v).reshape(3, 128, 512)
    for half in range(2):
        lanes = slice(256 * half, 256 * half + 256)
        both = jnp.concatenate([flux[1, :, lanes], flux[2, :, lanes]], axis=1)
        helm[:, :, lanes] = helm[:, :, lanes] + dot3(both, dyz, 0).reshape(3, 128, 256)
    stores = []
    for field, out in ((adv, adv_out), (helm, helm_out)):
        for c in range(3):
            local_sums(field, c)
            stores.append(pltpu.make_async_copy(field.at[c], out.at[c], sems.at[5 + len(stores)]))
            stores[-1].start()
    lane = lane_iota((32, 128))
    for c in range(3):
        xl[c] = jnp.where(lane < 64, adv[c, 0:32, 0:128], pltpu.roll(helm[c, 0:32, 0:128], 64, 1))
        xr[c] = jnp.where(lane < 64, pltpu.roll(adv[c, 96:128, 384:512], 64, 1), helm[c, 96:128, 384:512])
    for out, start, side in ((yl, 0, 0), (yr, 24, 1)):
        faces = []
        for field in (adv, helm):
            rows = field[...].reshape(12, 32, 512)[:, start : start + 8].reshape(96, 512)
            faces.append(pick(rows, pick_table(side)))
        out[...] = (faces[0] + pltpu.roll(faces[1], 64, 1)).reshape(3, 32, 128)
    for out, start, side in ((zl, 0, 2), (zr, 7, 3)):
        faces = []
        for field in (adv, helm):
            rows = field[...].reshape(48, 8, 512)[:, start]
            faces.append(pick(rows, pick_table(side)))
        out[...] = (faces[0] + pltpu.roll(faces[1], 64, 1)).reshape(3, 16, 128)
    for store in stores:
        store.wait()


def local_sums(field, c):
    lane = lane_iota((96, 128))
    upper = field[c, 0:96, 384:512]
    lower = field[c, 32:128, 0:128]
    field[c, 0:96, 384:512] = upper + jnp.where(lane >= 64, pltpu.roll(lower, 64, 1), 0.0)
    field[c, 32:128, 0:128] = lower + jnp.where(lane < 64, pltpu.roll(upper, 64, 1), 0.0)
    for tile in range(4):
        lanes = slice(128 * tile, 128 * tile + 128)
        y = field[c, :, lanes].reshape(4, 32, 128)
        below = y[:, 0:24].reshape(96, 128)
        above = y[:, 8:32].reshape(96, 128)
        j = lane // 8 % 8
        to_below = jnp.where(j == 7, pltpu.roll(above, 56, 1), 0.0).reshape(4, 24, 128)
        to_above = jnp.where(j == 0, pltpu.roll(below, 72, 1), 0.0).reshape(4, 24, 128)
        gap = jnp.zeros((4, 8, 128), f32)
        y = y + jnp.concatenate([to_below, gap], 1) + jnp.concatenate([gap, to_above], 1)
        z = y.reshape(16, 8, 128)
        lane_z = lane_iota((16, 8, 128)) % 8
        level = lax.broadcasted_iota(jnp.int32, (16, 8, 128), 1)
        from_below = pltpu.roll(pltpu.roll(z, 121, 2), 1, 1)
        from_above = pltpu.roll(pltpu.roll(z, 7, 2), 7, 1)
        z = z + jnp.where((lane_z == 0) & (level > 0), from_below, 0.0)
        z = z + jnp.where((lane_z == 7) & (level < 7), from_above, 0.0)
        field[c, :, lanes] = z.reshape(128, 128)


def y_face_kernel(xb, xa, yl_in, yr_in, yl, yr):
    lane = lane_iota((8, 128)) % 64
    for c in range(3):
        yl[c, 0:8] = yl_in[c, 0:8] + jnp.where(lane < 8, xb[c, 0:8], 0.0)
        yr[c, 0:8] = yr_in[c, 0:8] + jnp.where(lane < 8, pltpu.roll(xb[c, 24:32], 72, 1), 0.0)
        yl[c, 8:24] = yl_in[c, 8:24]
        yr[c, 8:24] = yr_in[c, 8:24]
        yl[c, 24:32] = yl_in[c, 24:32] + jnp.where(lane >= 56, pltpu.roll(xa[c, 0:8], 56, 1), 0.0)
        yr[c, 24:32] = yr_in[c, 24:32] + jnp.where(lane >= 56, xa[c, 24:32], 0.0)


def z_face_kernel(xb, xa, yb, ya, zl_in, zr_in, zl, zr):
    zl[...] = zl_in[...]
    zr[...] = zr_in[...]
    lane = lane_iota((1, 128)) % 8
    for out, level, side in ((zl, 0, 0), (zr, 7, 1)):
        for got, place in ((xb, 0), (xa, 1)):
            part = pick(got[...].reshape(96, 128), edge_table(side, place))
            for c in range(3):
                for b in range(4):
                    source = 32 * c + 8 * b + level
                    row = 12 * place + b
                    out[c, row : row + 1] += part[source : source + 1]
        for c in range(3):
            for a in range(4):
                source = 8 * a + level
                below = yb[c, source : source + 1]
                above = ya[c, source : source + 1]
                if side:
                    below = pltpu.roll(below, 121, 1)
                else:
                    above = pltpu.roll(above, 7, 1)
                out[c, 4 * a : 4 * a + 1] += jnp.where(lane == 0, below, 0.0)
                out[c, 4 * a + 3 : 4 * a + 4] += jnp.where(lane == 7, above, 0.0)


def end_kernel(adv_in, helm_in, xb, xa, yb, ya, zb, za, adv, helm, work, sems):
    loads, stores = [], []
    for c in range(3):
        for part, (source, target) in enumerate(((adv_in, adv), (helm_in, helm))):
            n = 2 * c + part
            loads.append(pltpu.make_async_copy(source.at[c], work.at[n], sems.at[n]))
            stores.append(pltpu.make_async_copy(work.at[n], target.at[c], sems.at[6 + n]))
            loads[n].start()
    lane = lane_iota((32, 128))
    level = lax.broadcasted_iota(jnp.int32, (16, 8, 512), 1)
    turned = [[got[...], pltpu.roll(got[...].reshape(-1, 128), 64, 1).reshape(got.shape)] for got in (xb, xa, yb, ya, zb, za)]
    for part in range(2):
        low_x, high_x = turned[0][part], turned[1][1 - part]
        wide = [spread(turned[2 + side][part].reshape(96, 128), pick_table(side)) for side in range(2)]
        ends = [spread(turned[4 + side][part].reshape(48, 128), pick_table(2 + side)) for side in range(2)]
        for c in range(3):
            n = 2 * c + part
            loads[n].wait()
            rows = slice(16 * c, 16 * c + 16)
            total = work[n].reshape(16, 8, 512)
            total = total + jnp.where(level == 0, ends[0][rows][:, None, :], 0.0)
            total = total + jnp.where(level == 7, ends[1][rows][:, None, :], 0.0)
            work[n] = total.reshape(128, 512)
            work[n, 0:32, 0:128] += jnp.where(lane < 64, low_x[c], 0.0)
            work[n, 96:128, 384:512] += jnp.where(lane >= 64, high_x[c], 0.0)
            for side, start in ((0, 0), (1, 24)):
                for a in range(4):
                    row = 32 * a + start
                    source = 32 * c + 8 * a
                    work[n, row : row + 8] += wide[side][source : source + 8]
            stores[n].start()
    for store in stores:
        store.wait()


def pack_kernel(coords, idents, counts, out):
    for source in range(32):
        for d in range(3):
            out[source, 4 * d : 4 * d + 4, 0] = coords[source, d]
    slot = lane_iota((32, 4))
    tags = jnp.where(slot < counts[...], idents[...], -1).astype(f32)
    out[:, 12, 0, 0:4] = tags


def table_kernel(vel, table):
    lane = lane_iota((128, 128))
    for c in range(3):
        for tile in range(4):
            x = vel[c, :, 128 * tile : 128 * tile + 128]
            high = x.astype(bf16).astype(f32)
            low = x - high
            for part in range(4):
                i, j_high = 2 * tile + part // 2, part % 2
                shift = -32 * part
                a = pltpu.roll(high, shift % 128, 1) if part else high
                b = pltpu.roll(low, (shift + 32) % 128, 1) if (shift + 32) % 128 else low
                d = pltpu.roll(high, (shift + 64) % 128, 1) if (shift + 64) % 128 else high
                row = (j_high * 3 + c) * 8 + i
                mixed = jnp.where(lane < 32, a, jnp.where(lane < 64, b, jnp.where(lane < 96, d, 0.0)))
                table[128 * row : 128 * row + 128] = mixed


def fibre_kernel(got_in, table, basis, got, out, live, tags, sem):
    load = pltpu.make_async_copy(got_in.at[:, 12, 0], tags, sem)
    load.start()
    load.wait()

    def ids(block):
        return tags[block // 4, block % 4]

    for slot in range(128 + UNROLL):
        live[slot] = 0

    def gather(block, count):
        live[count] = block
        return count + jnp.where(ids(block) >= 0.0, 1, 0)

    count = lax.fori_loop(0, 128, gather, 0, unroll=8)
    live[count] = 0

    def weights(position):
        value = basis[7]
        for place in range(7):
            value = value * (position - basis[place])
        return value

    def one(block):
        source = block // 4
        slot = block % 4
        elem = jnp.maximum(ids(block), 0.0).astype(jnp.int32)
        nodes = table[pl.ds(elem, 48, stride=128), :].astype(bf16)
        basis_x, basis_y, basis_z = (
            weights(jnp.broadcast_to(got[source, 4 * d + slot], (8, 128))) for d in range(3)
        )
        high = basis_z.astype(bf16).astype(f32)
        low = basis_z - high
        zero = jnp.zeros((8, 128), f32)
        columns = []
        for j in range(4):
            pieces = [zero] * 16
            pieces[j] = high
            pieces[4 + j] = high
            pieces[8 + j] = low
            columns.append(jnp.concatenate(pieces, 0).astype(bf16))
        sections = [mm(nodes, column) for column in columns]
        for c in range(3):
            total = jnp.zeros((8, 128), f32)
            for j in range(8):
                row = (j // 4 * 3 + c) * 8
                total = total + sections[j % 4][row : row + 8] * basis_y[j : j + 1]
            out[source, 4 * c + slot] = jnp.sum(total * basis_x, axis=0, keepdims=True)

    def group(step, carry):
        for u in range(UNROLL):
            one(live[step * UNROLL + u])
        return carry

    lax.fori_loop(0, (count + UNROLL - 1) // UNROLL, group, 0)


vmem = pl.BlockSpec(memory_space=pltpu.VMEM)
hbm = pl.BlockSpec(memory_space=pltpu.HBM)
anywhere = pl.BlockSpec(memory_space=pl.ANY)


def call(kernel, outs, args, specs=None, scratch=(), out_specs=None):
    out_specs = out_specs or [vmem] * len(outs)
    args = [
        pltpu.with_memory_space_constraint(arg, pltpu.HBM) if spec is hbm else arg
        for arg, spec in zip(args, specs or [vmem] * len(args))
    ]
    shapes = [
        pltpu.HBM(shape, f32) if spec is hbm else jax.ShapeDtypeStruct(shape, f32)
        for shape, spec in zip(outs, out_specs)
    ]
    return pl.pallas_call(
        kernel,
        out_shape=shapes,
        in_specs=specs or [vmem] * len(args),
        out_specs=out_specs,
        scratch_shapes=list(scratch),
        compiler_params=pltpu.CompilerParams(vmem_limit_bytes=VMEM_LIMIT),
        name=kernel.__name__,
    )(*args)


def swap(axis, left, right):
    size = lax.axis_size(axis)
    odd = lax.axis_index(axis) % 2 == 1
    even_pairs = [(i, i ^ 1) for i in range(size)]
    odd_pairs = [(i, ((i + 1) ^ 1) - 1) for i in range(1, size - 1)]
    first = lax.ppermute(jnp.where(odd, left, right), axis, even_pairs)
    second = lax.ppermute(jnp.where(odd, right, left), axis, odd_pairs)
    return jnp.where(odd, first, second), jnp.where(odd, second, first)


def body(velocity, viscosity, fibre_coords, fibre_elem, block_count, fibre_velocity):
    vel = velocity.reshape(3, 128, 512)
    visc = viscosity.reshape(128, 512)
    coords = fibre_coords.reshape(32, 4, 3, 128).transpose(0, 2, 1, 3)
    idents = fibre_elem.reshape(32, 4)
    counts = block_count.reshape(32, 1)
    own_velocity = fibre_velocity.reshape(32, 4, 3, 128).transpose(0, 2, 1, 3)
    live = lax.broadcasted_iota(jnp.int32, (32, 4), 1) < counts
    (packed,) = call(pack_kernel, [(32, 13, 1, 128)], (coords, idents, counts))
    got = lax.all_to_all(packed, "gz", split_axis=0, concat_axis=0, tiled=True)

    dx, dyz, mass = operator_tables()
    field = (3, 128, 512)
    y_face, z_face = (3, 32, 128), (3, 16, 128)
    adv, helm, xl, xr, yl, yr, zl, zr = call(
        fluid_kernel, [field, field] + [y_face] * 4 + [z_face] * 2, (vel, visc, dx, dyz, mass),
        specs=[hbm] * 5,
        out_specs=[hbm] * 2 + [vmem] * 6,
        scratch=[
            pltpu.VMEM((3, 384, 512), f32),
            pltpu.VMEM(field, f32),
            pltpu.VMEM(field, f32),
            pltpu.VMEM(field, f32),
            pltpu.VMEM((128, 512), f32),
            pltpu.VMEM(dx.shape, f32),
            pltpu.VMEM(dyz.shape, f32),
            pltpu.VMEM((1, 512), f32),
            pltpu.SemaphoreType.DMA((11,)),
        ],
    )
    (table,) = call(table_kernel, [(48 * 128, 128)], (vel,))
    xb, xa = swap("gx", xl, xr)
    yl, yr = call(y_face_kernel, [y_face] * 2, (xb, xa, yl, yr))
    yb, ya = swap("gy", yl, yr)
    got, yl = lax.optimization_barrier((got, yl))
    (values,) = call(
        fibre_kernel, [(32, 12, 1, 128)], (got, table, basis_table(), got),
        specs=[anywhere, vmem, vmem, vmem],
        scratch=[
            pltpu.SMEM((128 + 2 * UNROLL,), jnp.int32),
            pltpu.SMEM((32, 128), f32),
            pltpu.SemaphoreType.DMA,
        ],
    )
    values, yb, ya = lax.optimization_barrier((values, yb, ya))
    zl, zr = call(z_face_kernel, [z_face] * 2, (xb, xa, yb, ya, zl, zr))
    zb, za = swap("gz", zl, zr)
    adv, helm = call(
        end_kernel, [field, field], (adv, helm, xb, xa, yb, ya, zb, za),
        specs=[hbm] * 2 + [vmem] * 6, out_specs=[hbm] * 2,
        scratch=[
            pltpu.VMEM((6, 128, 512), f32),
            pltpu.SemaphoreType.DMA((12,)),
        ],
    )
    sampled = lax.all_to_all(values, "gz", split_axis=0, concat_axis=0, tiled=True).reshape(32, 3, 4, 128)
    relative = sampled - own_velocity
    factor = jnp.sqrt(1.0 + jnp.sum(relative * relative, axis=1, keepdims=True))
    drag = jnp.where(live[:, None, :, None], drag_scale * factor * relative, 0.0)
    drag = drag.transpose(0, 2, 1, 3).reshape(fibre_coords.shape)
    return adv.reshape(velocity.shape), helm.reshape(velocity.shape), drag


def solution(mesh):
    in_specs = (
        P(None, "gx", "gy", "gz", None),
        P("gx", "gy", "gz", None),
        P("gx", "gy", "gz", None, None, None, None),
        P("gx", "gy", "gz", None, None),
        P("gx", "gy", "gz", None),
        P("gx", "gy", "gz", None, None, None, None),
    )
    out_specs = (
        P(None, "gx", "gy", "gz", None),
        P(None, "gx", "gy", "gz", None),
        P("gx", "gy", "gz", None, None, None, None),
    )
    return jax.shard_map(body, mesh=mesh, in_specs=in_specs, out_specs=out_specs, check_vma=False)
```

```python
import jax
import jax.numpy as jnp
import numpy as np
from jax import lax
from jax.experimental import pallas as pl
from jax.experimental.pallas import tpu as pltpu
from jax.sharding import PartitionSpec as P

gll_points = (
    -1.0,
    -0.8717401485096066,
    -0.5917001814331423,
    -0.2092992179024789,
    0.2092992179024789,
    0.5917001814331423,
    0.8717401485096066,
    1.0,
)
gll_weights = (
    0.03571428571428571,
    0.2107042271435061,
    0.3411226924835044,
    0.4124587946587038,
    0.4124587946587038,
    0.3411226924835044,
    0.2107042271435061,
    0.03571428571428571,
)
helm_shift = 20.0
drag_scale = 0.5
UNROLL = 8
VMEM_LIMIT = 48 * 1024 * 1024
f32 = jnp.float32
bf16 = jnp.bfloat16


def derivative_table():
    points = list(gll_points)
    barycentric = [1.0] * 8
    for row in range(8):
        for other in range(8):
            if other != row:
                barycentric[row] = barycentric[row] / (points[row] - points[other])
    derivative = np.zeros((8, 8))
    for row in range(8):
        total = 0.0
        for other in range(8):
            if other != row:
                entry = barycentric[other] / barycentric[row] / (points[row] - points[other])
                derivative[row, other] = entry
                total = total + entry
        derivative[row, row] = -total
    return derivative


def operator_tables():
    derivative = derivative_table()
    identity = np.eye(8)
    kron_x = np.kron(np.kron(derivative, identity), identity)
    kron_y = np.kron(np.eye(4), np.kron(derivative, identity))
    kron_z = np.kron(np.eye(32), derivative)
    kron_yz = np.concatenate([kron_y, kron_z], 0)
    weights = np.asarray(gll_weights)
    mass = (weights[:, None, None] * weights[None, :, None] * weights[None, None, :]).reshape(1, 512)
    return (
        kron_x.astype(np.float32),
        kron_yz.astype(np.float32),
        mass.astype(np.float32),
    )


def pick_table(face):
    node = lax.broadcasted_iota(jnp.int32, (512, 128), 0)
    lane = lax.broadcasted_iota(jnp.int32, (512, 128), 1)
    i, j, k = node >> 6, (node >> 3) & 7, node & 7
    edge = 7 * (face % 2)
    if face < 2:
        hit = (j == edge) & (lane == i * 8 + k)
    else:
        hit = (k == edge) & (lane == i * 8 + j)
    return jnp.where(hit, 1.0, 0.0).astype(bf16)


def edge_table(side, place):
    source = lax.broadcasted_iota(jnp.int32, (128, 128), 0)
    lane = lax.broadcasted_iota(jnp.int32, (128, 128), 1)
    target = (source & 64) + 56 * place + ((source >> 3) & 7)
    hit = ((source & 7) == 7 * side) & (lane == target)
    return jnp.where(hit, 1.0, 0.0).astype(bf16)


def basis_rows():
    node = lax.broadcasted_iota(jnp.int32, (8, 128), 0)
    rows = []
    for place in range(7):
        value = jnp.full((8, 128), gll_points[place + 1], f32)
        for row in range(place + 1, 8):
            value = jnp.where(node == row, gll_points[place], value)
        rows.append(value)
    scales = jnp.ones((8, 128), f32)
    for row in range(8):
        scale = 1.0
        for other in range(8):
            if other != row:
                scale = scale / (gll_points[row] - gll_points[other])
        scales = jnp.where(node == row, scale, scales)
    return rows, scales


def split(x):
    high = x.astype(bf16)
    low = (x - high.astype(f32)).astype(bf16)
    return high, low


def mm(a, b, dims=((1,), (0,))):
    return lax.dot_general(a, b, (dims, ((), ())), preferred_element_type=f32)


def dot3(x, table, side):
    high, low = split(x)
    dims = ((1,), (side,))
    return mm(high, table[0], dims) + mm(high, table[1], dims) + mm(low, table[0], dims)


def pick(x, table):
    high, low = split(x)
    return mm(high, table) + mm(low, table)


def spread(x, table):
    high, low = split(x)
    dims = ((1,), (1,))
    return mm(high, table, dims) + mm(low, table, dims)


def lane_iota(shape):
    return lax.broadcasted_iota(jnp.int32, shape, len(shape) - 1)


def fluid_kernel(odds, vel_in, visc_in, dx_in, dyz_in, mass_in, adv_out, helm_out, x_work, y_out, z_out, table, flux, y_work, z_work, adv, helm, vel, visc, dx_ref, dyz_ref, mass_ref, sems):
    pairs = ((vel_in, vel), (dx_in, dx_ref), (dyz_in, dyz_ref), (visc_in, visc), (mass_in, mass_ref))
    loads = [pltpu.make_async_copy(a, b, sems.at[n]) for n, (a, b) in enumerate(pairs)]
    for load in loads:
        load.start()
    loads[0].wait()
    fill_table(vel, table, (0, 1))
    loads[1].wait()
    v = vel[...].reshape(384, 512)
    dx = split(dx_ref[...])
    flux[0] = dot3(v, dx, 1)
    loads[2].wait()
    dyz = split(dyz_ref[...])
    for half in range(2):
        lanes = slice(256 * half, 256 * half + 256)
        g = dot3(v[:, lanes], dyz, 1)
        flux[1, :, lanes] = g[:, :256]
        flux[2, :, lanes] = g[:, 256:]
    loads[3].wait()
    loads[4].wait()
    mass = mass_ref[...]
    weighted = mass * visc[...]
    for c in range(3):
        rows = slice(128 * c, 128 * c + 128)
        total = vel[0] * flux[0, rows] + vel[1] * flux[1, rows] + vel[2] * flux[2, rows]
        adv[c] = mass * total
        for d in range(3):
            flux[d, rows] = weighted * flux[d, rows]
    stiff = dot3(flux[0], dx, 0)
    helm[...] = (stiff + (helm_shift * mass) * v).reshape(3, 128, 512)
    for half in range(2):
        lanes = slice(256 * half, 256 * half + 256)
        both = jnp.concatenate([flux[1, :, lanes], flux[2, :, lanes]], axis=1)
        helm[:, :, lanes] = helm[:, :, lanes] + dot3(both, dyz, 0).reshape(3, 128, 256)
    stores = []
    for field, out in ((adv, adv_out), (helm, helm_out)):
        for c in range(3):
            local_sums(field, c)
            stores.append(pltpu.make_async_copy(field.at[c], out.at[c], sems.at[5 + len(stores)]))
            stores[-1].start()
    lane = lane_iota((32, 128))
    odd = odds[0]
    for c in range(3):
        left = jnp.where(lane < 64, adv[c, 0:32, 0:128], pltpu.roll(helm[c, 0:32, 0:128], 64, 1))
        right = jnp.where(lane < 64, pltpu.roll(adv[c, 96:128, 384:512], 64, 1), helm[c, 96:128, 384:512])
        x_work[1 - odd, c] = left
        x_work[odd, c] = right
    for out, start, side in ((y_work.at[0], 0, 0), (y_work.at[1], 24, 1)):
        faces = []
        for field in (adv, helm):
            rows = field[...].reshape(12, 32, 512)[:, start : start + 8].reshape(96, 512)
            faces.append(pick(rows, pick_table(side)))
        out[...] = (faces[0] + pltpu.roll(faces[1], 64, 1)).reshape(3, 32, 128)
    for out, start, side in ((z_work.at[0], 0, 2), (z_work.at[1], 7, 3)):
        faces = []
        for field in (adv, helm):
            rows = field[...].reshape(48, 8, 512)[:, start]
            faces.append(pick(rows, pick_table(side)))
        out[...] = (faces[0] + pltpu.roll(faces[1], 64, 1)).reshape(3, 16, 128)
    stores.append(pltpu.make_async_copy(y_work, y_out, sems.at[12]))
    stores[-1].start()
    stores.append(pltpu.make_async_copy(z_work, z_out, sems.at[13]))
    stores[-1].start()
    fill_table(vel, table, (2, 3))
    for store in stores:
        store.wait()


def local_sums(field, c):
    lane = lane_iota((96, 128))
    upper = field[c, 0:96, 384:512]
    lower = field[c, 32:128, 0:128]
    field[c, 0:96, 384:512] = upper + jnp.where(lane >= 64, pltpu.roll(lower, 64, 1), 0.0)
    field[c, 32:128, 0:128] = lower + jnp.where(lane < 64, pltpu.roll(upper, 64, 1), 0.0)
    for tile in range(4):
        lanes = slice(128 * tile, 128 * tile + 128)
        y = field[c, :, lanes].reshape(4, 32, 128)
        below = y[:, 0:24].reshape(96, 128)
        above = y[:, 8:32].reshape(96, 128)
        j = lane // 8 % 8
        to_below = jnp.where(j == 7, pltpu.roll(above, 56, 1), 0.0).reshape(4, 24, 128)
        to_above = jnp.where(j == 0, pltpu.roll(below, 72, 1), 0.0).reshape(4, 24, 128)
        gap = jnp.zeros((4, 8, 128), f32)
        y = y + jnp.concatenate([to_below, gap], 1) + jnp.concatenate([gap, to_above], 1)
        z = y.reshape(16, 8, 128)
        lane_z = lane_iota((16, 8, 128)) % 8
        level = lax.broadcasted_iota(jnp.int32, (16, 8, 128), 1)
        from_below = pltpu.roll(pltpu.roll(z, 121, 2), 1, 1)
        from_above = pltpu.roll(pltpu.roll(z, 7, 2), 7, 1)
        z = z + jnp.where((lane_z == 0) & (level > 0), from_below, 0.0)
        z = z + jnp.where((lane_z == 7) & (level < 7), from_above, 0.0)
        field[c, :, lanes] = z.reshape(128, 128)


def both_sides(odd, first, second):
    flag = jnp.full((8, 128), odd, jnp.int32) == 1

    def below(c, rows):
        flags = flag[: rows.stop - rows.start]
        return jnp.where(flags, first[c, rows], second[c, rows])

    def above(c, rows):
        flags = flag[: rows.stop - rows.start]
        return jnp.where(flags, second[c, rows], first[c, rows])

    return below, above


def y_face_kernel(odds, x1_in, x2_in, y_in, z_in, y1, y2, x1, x2, z, y_raw, sems):
    pairs = ((x1_in, x1), (x2_in, x2), (y_in, y_raw), (z_in, z))
    loads = [pltpu.make_async_copy(a, b, sems.at[n]) for n, (a, b) in enumerate(pairs)]
    for load in loads:
        load.start()
    for load in loads:
        load.wait()
    lane = lane_iota((8, 128)) % 64
    xb, xa = both_sides(odds[0], x1, x2)
    odd = jnp.full((8, 128), odds[1], jnp.int32) == 1
    head, tail = slice(0, 8), slice(24, 32)
    for c in range(3):
        extra = {
            (0, 0): jnp.where(lane < 8, xb(c, head), 0.0),
            (1, 0): jnp.where(lane < 8, pltpu.roll(xb(c, tail), 72, 1), 0.0),
            (0, 3): jnp.where(lane >= 56, pltpu.roll(xa(c, head), 56, 1), 0.0),
            (1, 3): jnp.where(lane >= 56, xa(c, tail), 0.0),
        }
        for a in range(4):
            rows = slice(8 * a, 8 * a + 8)
            left, right = y_raw[0, c, rows], y_raw[1, c, rows]
            if a in (0, 3):
                left = left + extra[0, a]
                right = right + extra[1, a]
            y1[c, rows] = jnp.where(odd, left, right)
            y2[c, rows] = jnp.where(odd, right, left)


def z_face_kernel(odds, x1, x2, y1, y2, z_raw, out1, out2, z):
    z[...] = z_raw[...]
    lane = lane_iota((1, 128)) % 8
    x_odd = jnp.full((96, 128), odds[0], jnp.int32) == 1
    x_first, x_second = x1[...].reshape(96, 128), x2[...].reshape(96, 128)
    xb, xa = jnp.where(x_odd, x_first, x_second), jnp.where(x_odd, x_second, x_first)
    yb, ya = both_sides(odds[1], y1, y2)
    for level, side in ((0, 0), (7, 1)):
        for got, place in ((xb, 0), (xa, 1)):
            part = pick(got, edge_table(side, place))
            for c in range(3):
                for b in range(4):
                    source = 32 * c + 8 * b + level
                    row = 12 * place + b
                    z[side, c, row : row + 1] += part[source : source + 1]
        for c in range(3):
            for a in range(4):
                row = slice(8 * a + level, 8 * a + level + 1)
                below, above = yb(c, row), ya(c, row)
                if side:
                    below = pltpu.roll(below, 121, 1)
                else:
                    above = pltpu.roll(above, 7, 1)
                z[side, c, 4 * a : 4 * a + 1] += jnp.where(lane == 0, below, 0.0)
                z[side, c, 4 * a + 3 : 4 * a + 4] += jnp.where(lane == 7, above, 0.0)
    odd = jnp.full((3, 16, 128), odds[2], jnp.int32) == 1
    out1[...] = jnp.where(odd, z[0], z[1])
    out2[...] = jnp.where(odd, z[1], z[0])


def sides(odd, first, second):
    rows = first.shape[0] * first.shape[1]
    flag = jnp.full((rows, 128), odd, jnp.int32) == 1
    one, two = first[...].reshape(rows, 128), second[...].reshape(rows, 128)
    below, above = jnp.where(flag, one, two), jnp.where(flag, two, one)
    return [[got, pltpu.roll(got, 64, 1)] for got in (below, above)]


def side_kernel(odds, adv_in, helm_in, x1, x2, y1, y2, work, sems):
    loads = []
    for c in range(3):
        for part, source in enumerate((adv_in, helm_in)):
            n = 3 * part + c
            loads.append(pltpu.make_async_copy(source.at[c], work.at[n], sems.at[n]))
            loads[-1].start()
    lane = lane_iota((32, 128))
    x_sides = sides(odds[0], x1, x2)
    y_sides = sides(odds[1], y1, y2)
    wide = [[spread(y_sides[side][part], pick_table(side)) for side in range(2)] for part in range(2)]
    for load in loads:
        load.wait()
    for part in range(2):
        for c in range(3):
            n = 3 * part + c
            faces = slice(32 * c, 32 * c + 32)
            work[n, 0:32, 0:128] += jnp.where(lane < 64, x_sides[0][part][faces], 0.0)
            work[n, 96:128, 384:512] += jnp.where(lane >= 64, x_sides[1][1 - part][faces], 0.0)
            for side, start in ((0, 0), (1, 24)):
                for a in range(4):
                    row = 32 * a + start
                    source = 32 * c + 8 * a
                    work[n, row : row + 8] += wide[part][side][source : source + 8]


def end_kernel(odds, work, z1, z2, adv, helm, done, sems):
    level = lax.broadcasted_iota(jnp.int32, (16, 8, 512), 1)
    z_sides = sides(odds[2], z1, z2)
    stores = []
    for part, target in enumerate((adv, helm)):
        ends = [spread(z_sides[side][part], pick_table(2 + side)) for side in range(2)]
        for c in range(3):
            n = 3 * part + c
            rows = slice(16 * c, 16 * c + 16)
            total = work[n].reshape(16, 8, 512)
            total = total + jnp.where(level == 0, ends[0][rows][:, None, :], 0.0)
            total = total + jnp.where(level == 7, ends[1][rows][:, None, :], 0.0)
            done[n] = total.reshape(128, 512)
            stores.append(pltpu.make_async_copy(done.at[n], target.at[c], sems.at[n]))
            stores[-1].start()
    for store in stores:
        store.wait()


def drag_kernel(counts, sampled, own, out):
    slot = lax.broadcasted_iota(jnp.int32, (4, 128), 0)
    for source in range(32):
        relative = [sampled[source, 4 * d : 4 * d + 4, 0] - own[source, d] for d in range(3)]
        square = relative[0] * relative[0] + relative[1] * relative[1] + relative[2] * relative[2]
        factor = jnp.where(slot < counts[source], drag_scale * jnp.sqrt(1.0 + square), 0.0)
        for d in range(3):
            out[source, d] = jnp.where(slot < counts[source], factor * relative[d], 0.0)


def pack_kernel(coords_in, idents_in, counts_in, out, coords, idents, counts, sems):
    pairs = ((coords_in, coords), (idents_in, idents), (counts_in, counts))
    loads = [pltpu.make_async_copy(a, b, sems.at[n]) for n, (a, b) in enumerate(pairs)]
    for load in loads:
        load.start()
    for load in loads:
        load.wait()
    slot = lax.broadcasted_iota(jnp.int32, (4, 32), 0)
    tags = jnp.where(slot < counts[...], idents[...], -1).astype(f32)
    tags = jnp.concatenate([tags[q : q + 1] for q in range(4)], axis=1)
    for source in range(32):
        for d in range(3):
            out[source, 4 * d : 4 * d + 4, 0] = coords[source, d]
        out[source, 12] = tags


def fill_table(vel, table, tiles):
    lane = lane_iota((128, 128))
    for c in range(3):
        for tile in tiles:
            x = vel[c, :, 128 * tile : 128 * tile + 128]
            high = x.astype(bf16).astype(f32)
            low = x - high
            for part in range(4):
                i, j_high = 2 * tile + part // 2, part % 2
                shift = -32 * part
                a = pltpu.roll(high, shift % 128, 1) if part else high
                b = pltpu.roll(low, (shift + 32) % 128, 1) if (shift + 32) % 128 else low
                d = pltpu.roll(high, (shift + 64) % 128, 1) if (shift + 64) % 128 else high
                row = (j_high * 3 + c) * 8 + i
                mixed = jnp.where(lane < 32, a, jnp.where(lane < 64, b, jnp.where(lane < 96, d, 0.0)))
                table[128 * row : 128 * row + 128] = mixed


def fibre_kernel(place, got_in, table, out_hbm, got, out, live, tags, sems):
    load_tags = pltpu.make_async_copy(got_in.at[:, 12, 0], tags, sems.at[0])
    load_tags.start()
    load_got = pltpu.make_async_copy(got_in, got, sems.at[1])
    load_got.start()
    load_tags.wait()
    me = place[0]

    def ids(block):
        return tags[block // 4, block % 4 * 32 + me]

    for slot in range(128 + UNROLL):
        live[slot] = 0

    def gather(block, count):
        live[count] = block
        return count + jnp.where(ids(block) >= 0.0, 1, 0)

    count = lax.fori_loop(0, 128, gather, 0, unroll=8)
    live[count] = 0
    load_got.wait()
    rows, scales = basis_rows()

    def weights(position):
        value = scales
        for row in rows:
            value = value * (position - row)
        return value

    def one(block):
        source = block // 4
        slot = block % 4
        elem = jnp.maximum(ids(block), 0.0).astype(jnp.int32)
        nodes = table[pl.ds(elem, 48, stride=128), :].astype(bf16)
        basis_x, basis_y, basis_z = (
            weights(jnp.broadcast_to(got[source, 4 * d + slot], (8, 128))) for d in range(3)
        )
        high = basis_z.astype(bf16).astype(f32)
        low = basis_z - high
        zero = jnp.zeros((8, 128), f32)
        columns = []
        for j in range(4):
            pieces = [zero] * 16
            pieces[j] = high
            pieces[4 + j] = high
            pieces[8 + j] = low
            columns.append(jnp.concatenate(pieces, 0).astype(bf16))
        sections = [mm(nodes, column) for column in columns]
        for c in range(3):
            total = jnp.zeros((8, 128), f32)
            for j in range(8):
                top = (j // 4 * 3 + c) * 8
                total = total + sections[j % 4][top : top + 8] * basis_y[j : j + 1]
            out[source, 4 * c + slot] = jnp.sum(total * basis_x, axis=0, keepdims=True)

    def group(step, carry):
        for u in range(UNROLL):
            one(live[step * UNROLL + u])
        return carry

    lax.fori_loop(0, (count + UNROLL - 1) // UNROLL, group, 0)
    store = pltpu.make_async_copy(out, out_hbm, sems.at[2])
    store.start()
    store.wait()


vmem = pl.BlockSpec(memory_space=pltpu.VMEM)
hbm = pl.BlockSpec(memory_space=pltpu.HBM)
smem = pl.BlockSpec(memory_space=pltpu.SMEM)


def call(kernel, outs, args, specs=None, scratch=(), out_specs=None):
    out_specs = out_specs or [vmem] * len(outs)
    args = [
        pltpu.with_memory_space_constraint(arg, pltpu.HBM) if spec is hbm else arg
        for arg, spec in zip(args, specs or [vmem] * len(args))
    ]
    shapes = [
        pltpu.HBM(shape, f32) if spec is hbm else jax.ShapeDtypeStruct(shape, f32)
        for shape, spec in zip(outs, out_specs)
    ]
    return pl.pallas_call(
        kernel,
        out_shape=shapes,
        in_specs=specs or [vmem] * len(args),
        out_specs=out_specs,
        scratch_shapes=list(scratch),
        compiler_params=pltpu.CompilerParams(vmem_limit_bytes=VMEM_LIMIT),
        name=kernel.__name__,
    )(*args)


def swap(axis, first, second):
    size = lax.axis_size(axis)
    even_pairs = [(i, i ^ 1) for i in range(size)]
    odd_pairs = [(i, ((i + 1) ^ 1) - 1) for i in range(1, size - 1)]
    return lax.ppermute(first, axis, even_pairs), lax.ppermute(second, axis, odd_pairs)


def body(velocity, viscosity, fibre_coords, fibre_elem, block_count, fibre_velocity):
    vel = velocity.reshape(3, 128, 512)
    visc = viscosity.reshape(128, 512)
    coords = fibre_coords.reshape(32, 4, 3, 128).transpose(0, 2, 1, 3)
    idents = fibre_elem.reshape(32, 4).transpose(1, 0)
    counts = block_count.reshape(32)
    own_velocity = fibre_velocity.reshape(32, 4, 3, 128).transpose(0, 2, 1, 3)
    odds = jnp.stack([lax.axis_index(axis) % 2 for axis in ("gx", "gy", "gz")]).astype(jnp.int32)
    place = lax.axis_index("gz").astype(jnp.int32).reshape(1)
    (packed,) = call(
        pack_kernel, [(32, 13, 1, 128)], (coords, idents, counts.reshape(1, 32)), specs=[hbm] * 3,
        scratch=[
            pltpu.VMEM((32, 3, 4, 128), f32),
            pltpu.VMEM((4, 32), jnp.int32),
            pltpu.VMEM((1, 32), jnp.int32),
            pltpu.SemaphoreType.DMA((3,)),
        ],
    )
    got = lax.all_to_all(packed, "gz", split_axis=0, concat_axis=0, tiled=True)

    dx, dyz, mass = operator_tables()
    field = (3, 128, 512)
    y_face, z_face = (3, 32, 128), (3, 16, 128)
    y_pair, z_pair = (2,) + y_face, (2,) + z_face
    adv, helm, x_sends, y_raw, z_raw, table = call(
        fluid_kernel, [field, field, y_pair, y_pair, z_pair, (48 * 128, 128)], (odds, vel, visc, dx, dyz, mass),
        specs=[smem] + [hbm] * 5,
        out_specs=[hbm] * 2 + [vmem] + [hbm] * 2 + [vmem],
        scratch=[
            pltpu.VMEM((3, 384, 512), f32),
            pltpu.VMEM(y_pair, f32),
            pltpu.VMEM(z_pair, f32),
            pltpu.VMEM(field, f32),
            pltpu.VMEM(field, f32),
            pltpu.VMEM(field, f32),
            pltpu.VMEM((128, 512), f32),
            pltpu.VMEM(dx.shape, f32),
            pltpu.VMEM(dyz.shape, f32),
            pltpu.VMEM((1, 512), f32),
            pltpu.SemaphoreType.DMA((14,)),
        ],
    )
    x1, x2 = swap("gx", x_sends[0], x_sends[1])
    got, y_raw = lax.optimization_barrier((got, y_raw))
    (values,) = call(
        fibre_kernel, [(32, 12, 1, 128)], (place, got, table),
        specs=[smem, hbm, vmem], out_specs=[hbm],
        scratch=[
            pltpu.VMEM((32, 13, 1, 128), f32),
            pltpu.VMEM((32, 12, 1, 128), f32),
            pltpu.SMEM((128 + 2 * UNROLL,), jnp.int32),
            pltpu.SMEM((32, 128), f32),
            pltpu.SemaphoreType.DMA((3,)),
        ],
    )
    values, x1, x2 = lax.optimization_barrier((values, x1, x2))
    sampled = lax.all_to_all(values, "gz", split_axis=0, concat_axis=0, tiled=True)
    y1, y2, x1, x2, z_raw = call(
        y_face_kernel, [y_face] * 4 + [z_pair], (odds, x1, x2, y_raw, z_raw), specs=[smem] + [hbm] * 4,
        scratch=[pltpu.VMEM(y_pair, f32), pltpu.SemaphoreType.DMA((4,))],
    )
    y1, y2 = swap("gy", y1, y2)
    z1, z2 = call(
        z_face_kernel, [z_face] * 2, (odds, x1, x2, y1, y2, z_raw), specs=[smem] + [vmem] * 5,
        scratch=[pltpu.VMEM(z_pair, f32)],
    )
    z1, z2 = swap("gz", z1, z2)
    (work,) = call(
        side_kernel, [(6, 128, 512)], (odds, adv, helm, x1, x2, y1, y2), specs=[smem, hbm, hbm] + [vmem] * 4,
        scratch=[pltpu.SemaphoreType.DMA((6,))],
    )
    adv, helm = call(
        end_kernel, [field, field], (odds, work, z1, z2), specs=[smem] + [vmem] * 3, out_specs=[hbm] * 2,
        scratch=[pltpu.VMEM((6, 128, 512), f32), pltpu.SemaphoreType.DMA((6,))],
    )
    (drag,) = call(
        drag_kernel, [(32, 3, 4, 128)], (counts, sampled, own_velocity), specs=[smem, vmem, vmem]
    )
    drag = drag.transpose(0, 2, 1, 3).reshape(fibre_coords.shape)
    return adv.reshape(velocity.shape), helm.reshape(velocity.shape), drag


def solution(mesh):
    in_specs = (
        P(None, "gx", "gy", "gz", None),
        P("gx", "gy", "gz", None),
        P("gx", "gy", "gz", None, None, None, None),
        P("gx", "gy", "gz", None, None),
        P("gx", "gy", "gz", None),
        P("gx", "gy", "gz", None, None, None, None),
    )
    out_specs = (
        P(None, "gx", "gy", "gz", None),
        P(None, "gx", "gy", "gz", None),
        P("gx", "gy", "gz", None, None, None, None),
    )
    return jax.shard_map(body, mesh=mesh, in_specs=in_specs, out_specs=out_specs, check_vma=False)
```

```python
import jax
import jax.numpy as jnp
import numpy as np
from jax import lax
from jax.experimental import pallas as pl
from jax.experimental.pallas import tpu as pltpu
from jax.sharding import PartitionSpec as P

gll_points = (
    -1.0,
    -0.8717401485096066,
    -0.5917001814331423,
    -0.2092992179024789,
    0.2092992179024789,
    0.5917001814331423,
    0.8717401485096066,
    1.0,
)
gll_weights = (
    0.03571428571428571,
    0.2107042271435061,
    0.3411226924835044,
    0.4124587946587038,
    0.4124587946587038,
    0.3411226924835044,
    0.2107042271435061,
    0.03571428571428571,
)
helm_shift = 20.0
drag_scale = 0.5
UNROLL = 8
VMEM_LIMIT = 48 * 1024 * 1024
f32 = jnp.float32
bf16 = jnp.bfloat16


def derivative_table():
    points = list(gll_points)
    barycentric = [1.0] * 8
    for row in range(8):
        for other in range(8):
            if other != row:
                barycentric[row] = barycentric[row] / (points[row] - points[other])
    derivative = np.zeros((8, 8))
    for row in range(8):
        total = 0.0
        for other in range(8):
            if other != row:
                entry = barycentric[other] / barycentric[row] / (points[row] - points[other])
                derivative[row, other] = entry
                total = total + entry
        derivative[row, row] = -total
    return derivative


def operator_rows():
    derivative = derivative_table()
    lanes = np.arange(128)
    along_x = np.zeros((8, 4, 128))
    for half in range(2):
        along_x[:, :, 64 * half : 64 * half + 64] = derivative[:, half::2, None]
    along_y = derivative[:, lanes // 8 % 8]
    along_z = derivative[:, lanes % 8]
    rows = np.concatenate([along_x.reshape(32, 128), along_y, along_z]).astype(np.float32)
    weights = np.asarray(gll_weights)
    mass = (weights[:, None, None] * weights[None, :, None] * weights[None, None, :]).reshape(4, 128)
    mass = np.concatenate([mass, np.zeros((4, 128))]).astype(np.float32)
    return np.concatenate([rows, mass])


def fill_operators(rows, dx, dyz):
    row = lax.broadcasted_iota(jnp.int32, (64, 128), 0)
    lane = lax.broadcasted_iota(jnp.int32, (64, 128), 1)
    same = (row & 63) == (lane & 63)
    for a in range(8):
        for tile in range(4):
            values = jnp.where(same, rows[4 * a + tile : 4 * a + tile + 1], 0.0)
            high, low = split(values)
            dx[0, 64 * a : 64 * a + 64, 128 * tile : 128 * tile + 128] = high
            dx[1, 64 * a : 64 * a + 64, 128 * tile : 128 * tile + 128] = low
    row = lax.broadcasted_iota(jnp.int32, (128, 128), 0)
    lane = lax.broadcasted_iota(jnp.int32, (128, 128), 1)
    along_y = jnp.concatenate([jnp.broadcast_to(rows[32 + j % 8 : 33 + j % 8], (8, 128)) for j in range(16)], 0)
    along_z = jnp.concatenate([rows[40:48]] * 16, 0)
    along_y = jnp.where(((row ^ lane) & 71) == 0, along_y, 0.0)
    along_z = jnp.where((row >> 3) == (lane >> 3), along_z, 0.0)
    empty = jnp.zeros((128, 128), bf16)
    for start, values in ((0, along_y), (256, along_z)):
        for n, part in enumerate(split(values)):
            dyz[n, start : start + 128, 0:128] = part
            dyz[n, start : start + 128, 128:256] = empty
            dyz[n, start + 128 : start + 256, 0:128] = empty
            dyz[n, start + 128 : start + 256, 128:256] = part


def pick_table(face):
    node = lax.broadcasted_iota(jnp.int32, (512, 128), 0)
    lane = lax.broadcasted_iota(jnp.int32, (512, 128), 1)
    i, j, k = node >> 6, (node >> 3) & 7, node & 7
    edge = 7 * (face % 2)
    if face < 2:
        hit = (j == edge) & (lane == i * 8 + k)
    else:
        hit = (k == edge) & (lane == i * 8 + j)
    return jnp.where(hit, 1.0, 0.0).astype(bf16)


def edge_table(side, place):
    source = lax.broadcasted_iota(jnp.int32, (128, 128), 0)
    lane = lax.broadcasted_iota(jnp.int32, (128, 128), 1)
    target = (source & 64) + 56 * place + ((source >> 3) & 7)
    hit = ((source & 7) == 7 * side) & (lane == target)
    return jnp.where(hit, 1.0, 0.0).astype(bf16)


def basis_rows():
    node = lax.broadcasted_iota(jnp.int32, (8, 128), 0)
    rows = []
    for place in range(7):
        value = jnp.full((8, 128), gll_points[place + 1], f32)
        for row in range(place + 1, 8):
            value = jnp.where(node == row, gll_points[place], value)
        rows.append(value)
    scales = jnp.ones((8, 128), f32)
    for row in range(8):
        scale = 1.0
        for other in range(8):
            if other != row:
                scale = scale / (gll_points[row] - gll_points[other])
        scales = jnp.where(node == row, scale, scales)
    return rows, scales


def split(x):
    high = x.astype(bf16)
    low = (x - high.astype(f32)).astype(bf16)
    return high, low


def mm(a, b, dims=((1,), (0,))):
    return lax.dot_general(a, b, (dims, ((), ())), preferred_element_type=f32)


def dot3(x, table, side):
    high, low = split(x)
    dims = ((1,), (side,))
    return mm(high, table[0], dims) + mm(high, table[1], dims) + mm(low, table[0], dims)


def pick(x, table):
    high, low = split(x)
    return mm(high, table) + mm(low, table)


def spread(x, table):
    high, low = split(x)
    dims = ((1,), (1,))
    return mm(high, table, dims) + mm(low, table, dims)


def lane_iota(shape):
    return lax.broadcasted_iota(jnp.int32, shape, len(shape) - 1)


def fluid_kernel(vel_in, visc_in, rows_in, adv_out, helm_out, x_work, y_out, z_out, table, flux, y_work, z_work, adv, helm, vel, visc, rows, dx, dyz, sems):
    pairs = ((rows_in, rows), (vel_in, vel), (visc_in, visc))
    loads = [pltpu.make_async_copy(a, b, sems.at[n]) for n, (a, b) in enumerate(pairs)]
    for load in loads:
        load.start()
    loads[0].wait()
    fill_operators(rows, dx, dyz)
    loads[1].wait()
    v = vel[...].reshape(384, 512)
    flux[0] = dot3(v, dx, 1)
    for half in range(2):
        lanes = slice(256 * half, 256 * half + 256)
        g = dot3(v[:, lanes], dyz, 1)
        flux[1, :, lanes] = g[:, :256]
        flux[2, :, lanes] = g[:, 256:]
    loads[2].wait()
    mass = jnp.concatenate([rows[48 + tile : 49 + tile] for tile in range(4)], 1)
    weighted = mass * visc[...]
    for c in range(3):
        rows = slice(128 * c, 128 * c + 128)
        total = vel[0] * flux[0, rows] + vel[1] * flux[1, rows] + vel[2] * flux[2, rows]
        adv[c] = mass * total
        for d in range(3):
            flux[d, rows] = weighted * flux[d, rows]
    stiff = dot3(flux[0], dx, 0)
    helm[...] = (stiff + (helm_shift * mass) * v).reshape(3, 128, 512)
    for half in range(2):
        lanes = slice(256 * half, 256 * half + 256)
        both = jnp.concatenate([flux[1, :, lanes], flux[2, :, lanes]], axis=1)
        helm[:, :, lanes] = helm[:, :, lanes] + dot3(both, dyz, 0).reshape(3, 128, 256)
    stores = []
    for field, out in ((adv, adv_out), (helm, helm_out)):
        for c in range(3):
            local_sums(field, c)
            stores.append(pltpu.make_async_copy(field.at[c], out.at[c], sems.at[5 + len(stores)]))
            stores[-1].start()
    lane = lane_iota((32, 128))
    odd = lax.axis_index("gx") % 2
    for c in range(3):
        left = jnp.where(lane < 64, adv[c, 0:32, 0:128], pltpu.roll(helm[c, 0:32, 0:128], 64, 1))
        right = jnp.where(lane < 64, pltpu.roll(adv[c, 96:128, 384:512], 64, 1), helm[c, 96:128, 384:512])
        x_work[1 - odd, c] = left
        x_work[odd, c] = right
    for out, start, side in ((y_work.at[0], 0, 0), (y_work.at[1], 24, 1)):
        faces = []
        for field in (adv, helm):
            rows = field[...].reshape(12, 32, 512)[:, start : start + 8].reshape(96, 512)
            faces.append(pick(rows, pick_table(side)))
        out[...] = (faces[0] + pltpu.roll(faces[1], 64, 1)).reshape(3, 32, 128)
    for out, start, side in ((z_work.at[0], 0, 2), (z_work.at[1], 7, 3)):
        faces = []
        for field in (adv, helm):
            rows = field[...].reshape(48, 8, 512)[:, start]
            faces.append(pick(rows, pick_table(side)))
        out[...] = (faces[0] + pltpu.roll(faces[1], 64, 1)).reshape(3, 16, 128)
    stores.append(pltpu.make_async_copy(y_work, y_out, sems.at[12]))
    stores[-1].start()
    stores.append(pltpu.make_async_copy(z_work, z_out, sems.at[13]))
    stores[-1].start()
    fill_table(vel, table, range(4))
    for store in stores:
        store.wait()


def local_sums(field, c):
    lane = lane_iota((96, 128))
    upper = field[c, 0:96, 384:512]
    lower = field[c, 32:128, 0:128]
    field[c, 0:96, 384:512] = upper + jnp.where(lane >= 64, pltpu.roll(lower, 64, 1), 0.0)
    field[c, 32:128, 0:128] = lower + jnp.where(lane < 64, pltpu.roll(upper, 64, 1), 0.0)
    for tile in range(4):
        lanes = slice(128 * tile, 128 * tile + 128)
        y = field[c, :, lanes].reshape(4, 32, 128)
        below = y[:, 0:24].reshape(96, 128)
        above = y[:, 8:32].reshape(96, 128)
        j = lane // 8 % 8
        to_below = jnp.where(j == 7, pltpu.roll(above, 56, 1), 0.0).reshape(4, 24, 128)
        to_above = jnp.where(j == 0, pltpu.roll(below, 72, 1), 0.0).reshape(4, 24, 128)
        gap = jnp.zeros((4, 8, 128), f32)
        y = y + jnp.concatenate([to_below, gap], 1) + jnp.concatenate([gap, to_above], 1)
        z = y.reshape(16, 8, 128)
        lane_z = lane_iota((16, 8, 128)) % 8
        level = lax.broadcasted_iota(jnp.int32, (16, 8, 128), 1)
        from_below = pltpu.roll(pltpu.roll(z, 121, 2), 1, 1)
        from_above = pltpu.roll(pltpu.roll(z, 7, 2), 7, 1)
        z = z + jnp.where((lane_z == 0) & (level > 0), from_below, 0.0)
        z = z + jnp.where((lane_z == 7) & (level < 7), from_above, 0.0)
        field[c, :, lanes] = z.reshape(128, 128)


def both_sides(odd, first, second):
    flag = jnp.full((8, 128), odd, jnp.int32) == 1

    def below(c, rows):
        flags = flag[: rows.stop - rows.start]
        return jnp.where(flags, first[c, rows], second[c, rows])

    def above(c, rows):
        flags = flag[: rows.stop - rows.start]
        return jnp.where(flags, second[c, rows], first[c, rows])

    return below, above


def y_face_kernel(x1_in, x2_in, y_in, z_in, y1, y2, x1, x2, z, y_raw, sems):
    pairs = ((x1_in, x1), (x2_in, x2), (y_in, y_raw), (z_in, z))
    loads = [pltpu.make_async_copy(a, b, sems.at[n]) for n, (a, b) in enumerate(pairs)]
    for load in loads:
        load.start()
    for load in loads:
        load.wait()
    lane = lane_iota((8, 128)) % 64
    xb, xa = both_sides(lax.axis_index("gx") % 2, x1, x2)
    odd = jnp.full((8, 128), lax.axis_index("gy") % 2, jnp.int32) == 1
    head, tail = slice(0, 8), slice(24, 32)
    for c in range(3):
        extra = {
            (0, 0): jnp.where(lane < 8, xb(c, head), 0.0),
            (1, 0): jnp.where(lane < 8, pltpu.roll(xb(c, tail), 72, 1), 0.0),
            (0, 3): jnp.where(lane >= 56, pltpu.roll(xa(c, head), 56, 1), 0.0),
            (1, 3): jnp.where(lane >= 56, xa(c, tail), 0.0),
        }
        for a in range(4):
            rows = slice(8 * a, 8 * a + 8)
            left, right = y_raw[0, c, rows], y_raw[1, c, rows]
            if a in (0, 3):
                left = left + extra[0, a]
                right = right + extra[1, a]
            y1[c, rows] = jnp.where(odd, left, right)
            y2[c, rows] = jnp.where(odd, right, left)


def z_face_kernel(x1, x2, y1, y2, z_raw, out1, out2, z):
    z[...] = z_raw[...]
    lane = lane_iota((1, 128)) % 8
    x_odd = jnp.full((96, 128), lax.axis_index("gx") % 2, jnp.int32) == 1
    x_first, x_second = x1[...].reshape(96, 128), x2[...].reshape(96, 128)
    xb, xa = jnp.where(x_odd, x_first, x_second), jnp.where(x_odd, x_second, x_first)
    yb, ya = both_sides(lax.axis_index("gy") % 2, y1, y2)
    for level, side in ((0, 0), (7, 1)):
        for got, place in ((xb, 0), (xa, 1)):
            part = pick(got, edge_table(side, place))
            for c in range(3):
                for b in range(4):
                    source = 32 * c + 8 * b + level
                    row = 12 * place + b
                    z[side, c, row : row + 1] += part[source : source + 1]
        for c in range(3):
            for a in range(4):
                row = slice(8 * a + level, 8 * a + level + 1)
                below, above = yb(c, row), ya(c, row)
                if side:
                    below = pltpu.roll(below, 121, 1)
                else:
                    above = pltpu.roll(above, 7, 1)
                z[side, c, 4 * a : 4 * a + 1] += jnp.where(lane == 0, below, 0.0)
                z[side, c, 4 * a + 3 : 4 * a + 4] += jnp.where(lane == 7, above, 0.0)
    odd = jnp.full((3, 16, 128), lax.axis_index("gz") % 2, jnp.int32) == 1
    out1[...] = jnp.where(odd, z[0], z[1])
    out2[...] = jnp.where(odd, z[1], z[0])


def sides(odd, first, second):
    rows = first.shape[0] * first.shape[1]
    flag = jnp.full((rows, 128), odd, jnp.int32) == 1
    one, two = first[...].reshape(rows, 128), second[...].reshape(rows, 128)
    below, above = jnp.where(flag, one, two), jnp.where(flag, two, one)
    return [[got, pltpu.roll(got, 64, 1)] for got in (below, above)]


def side_kernel(adv_in, helm_in, x1, x2, y1, y2, work, sems):
    loads = []
    for c in range(3):
        for part, source in enumerate((adv_in, helm_in)):
            n = 3 * part + c
            loads.append(pltpu.make_async_copy(source.at[c], work.at[n], sems.at[n]))
            loads[-1].start()
    lane = lane_iota((32, 128))
    x_sides = sides(lax.axis_index("gx") % 2, x1, x2)
    y_sides = sides(lax.axis_index("gy") % 2, y1, y2)
    wide = [[spread(y_sides[side][part], pick_table(side)) for side in range(2)] for part in range(2)]
    for load in loads:
        load.wait()
    for part in range(2):
        for c in range(3):
            n = 3 * part + c
            faces = slice(32 * c, 32 * c + 32)
            work[n, 0:32, 0:128] += jnp.where(lane < 64, x_sides[0][part][faces], 0.0)
            work[n, 96:128, 384:512] += jnp.where(lane >= 64, x_sides[1][1 - part][faces], 0.0)
            for side, start in ((0, 0), (1, 24)):
                for a in range(4):
                    row = 32 * a + start
                    source = 32 * c + 8 * a
                    work[n, row : row + 8] += wide[part][side][source : source + 8]


def end_kernel(work, z1, z2, adv, helm, done, sems):
    level = lax.broadcasted_iota(jnp.int32, (16, 8, 512), 1)
    z_sides = sides(lax.axis_index("gz") % 2, z1, z2)
    stores = []
    for part, target in enumerate((adv, helm)):
        ends = [spread(z_sides[side][part], pick_table(2 + side)) for side in range(2)]
        for c in range(3):
            n = 3 * part + c
            rows = slice(16 * c, 16 * c + 16)
            total = work[n].reshape(16, 8, 512)
            total = total + jnp.where(level == 0, ends[0][rows][:, None, :], 0.0)
            total = total + jnp.where(level == 7, ends[1][rows][:, None, :], 0.0)
            done[n] = total.reshape(128, 512)
            stores.append(pltpu.make_async_copy(done.at[n], target.at[c], sems.at[n]))
            stores[-1].start()
    for store in stores:
        store.wait()


def drag_kernel(counts, sampled, own, out):
    slot = lax.broadcasted_iota(jnp.int32, (4, 128), 0)
    for source in range(32):
        relative = [sampled[source, 4 * d : 4 * d + 4, 0] - own[source, d] for d in range(3)]
        square = relative[0] * relative[0] + relative[1] * relative[1] + relative[2] * relative[2]
        factor = jnp.where(slot < counts[source], drag_scale * jnp.sqrt(1.0 + square), 0.0)
        for d in range(3):
            out[source, d] = jnp.where(slot < counts[source], factor * relative[d], 0.0)


def pack_kernel(coords_in, idents_in, counts_in, out, coords, idents, counts, sems):
    pairs = ((coords_in, coords), (idents_in, idents), (counts_in, counts))
    loads = [pltpu.make_async_copy(a, b, sems.at[n]) for n, (a, b) in enumerate(pairs)]
    for load in loads:
        load.start()
    for load in loads:
        load.wait()
    slot = lax.broadcasted_iota(jnp.int32, (4, 32), 0)
    tags = jnp.where(slot < counts[...], idents[...], -1).astype(f32)
    tags = jnp.concatenate([tags[q : q + 1] for q in range(4)], axis=1)
    for source in range(32):
        for d in range(3):
            out[source, 4 * d : 4 * d + 4, 0] = coords[source, d]
        out[source, 12] = tags


def fill_table(vel, table, tiles):
    lane = lane_iota((128, 128))
    for c in range(3):
        for tile in tiles:
            x = vel[c, :, 128 * tile : 128 * tile + 128]
            high = x.astype(bf16).astype(f32)
            low = x - high
            for part in range(4):
                i, j_high = 2 * tile + part // 2, part % 2
                shift = -32 * part
                a = pltpu.roll(high, shift % 128, 1) if part else high
                b = pltpu.roll(low, (shift + 32) % 128, 1) if (shift + 32) % 128 else low
                d = pltpu.roll(high, (shift + 64) % 128, 1) if (shift + 64) % 128 else high
                row = (j_high * 3 + c) * 8 + i
                mixed = jnp.where(lane < 32, a, jnp.where(lane < 64, b, jnp.where(lane < 96, d, 0.0)))
                table[128 * row : 128 * row + 128] = mixed


def fibre_kernel(got, table, out_hbm, out, live, tags, sems):
    load_tags = pltpu.make_async_copy(got.at[:, 12, 0], tags, sems.at[0])
    load_tags.start()
    load_tags.wait()
    me = lax.axis_index("gz")

    def ids(block):
        return tags[block // 4, block % 4 * 32 + me]

    for slot in range(128 + UNROLL):
        live[slot] = 0

    def gather(block, count):
        live[count] = block
        return count + jnp.where(ids(block) >= 0.0, 1, 0)

    count = lax.fori_loop(0, 128, gather, 0, unroll=8)
    live[count] = 0
    rows, scales = basis_rows()

    def weights(position):
        value = scales
        for row in rows:
            value = value * (position - row)
        return value

    def one(block):
        source = block // 4
        slot = block % 4
        elem = jnp.maximum(ids(block), 0.0).astype(jnp.int32)
        nodes = table[pl.ds(elem, 48, stride=128), :].astype(bf16)
        basis_x, basis_y, basis_z = (
            weights(jnp.broadcast_to(got[source, 4 * d + slot], (8, 128))) for d in range(3)
        )
        high = basis_z.astype(bf16).astype(f32)
        low = basis_z - high
        zero = jnp.zeros((8, 128), f32)
        columns = []
        for j in range(4):
            pieces = [zero] * 16
            pieces[j] = high
            pieces[4 + j] = high
            pieces[8 + j] = low
            columns.append(jnp.concatenate(pieces, 0).astype(bf16))
        sections = [mm(nodes, column) for column in columns]
        for c in range(3):
            total = jnp.zeros((8, 128), f32)
            for j in range(8):
                top = (j // 4 * 3 + c) * 8
                total = total + sections[j % 4][top : top + 8] * basis_y[j : j + 1]
            out[source, 4 * c + slot] = jnp.sum(total * basis_x, axis=0, keepdims=True)

    def group(step, carry):
        for u in range(UNROLL):
            one(live[step * UNROLL + u])
        return carry

    lax.fori_loop(0, (count + UNROLL - 1) // UNROLL, group, 0)
    store = pltpu.make_async_copy(out, out_hbm, sems.at[1])
    store.start()
    store.wait()


vmem = pl.BlockSpec(memory_space=pltpu.VMEM)
hbm = pl.BlockSpec(memory_space=pltpu.HBM)
smem = pl.BlockSpec(memory_space=pltpu.SMEM)


def call(kernel, outs, args, specs=None, scratch=(), out_specs=None):
    out_specs = out_specs or [vmem] * len(outs)
    args = [
        pltpu.with_memory_space_constraint(arg, pltpu.HBM) if spec is hbm else arg
        for arg, spec in zip(args, specs or [vmem] * len(args))
    ]
    shapes = [
        pltpu.HBM(shape, f32) if spec is hbm else jax.ShapeDtypeStruct(shape, f32)
        for shape, spec in zip(outs, out_specs)
    ]
    return pl.pallas_call(
        kernel,
        out_shape=shapes,
        in_specs=specs or [vmem] * len(args),
        out_specs=out_specs,
        scratch_shapes=list(scratch),
        compiler_params=pltpu.CompilerParams(vmem_limit_bytes=VMEM_LIMIT),
        name=kernel.__name__,
    )(*args)


def swap(axis, first, second):
    size = lax.axis_size(axis)
    even_pairs = [(i, i ^ 1) for i in range(size)]
    odd_pairs = [(i, ((i + 1) ^ 1) - 1) for i in range(1, size - 1)]
    return lax.ppermute(first, axis, even_pairs), lax.ppermute(second, axis, odd_pairs)


def body(velocity, viscosity, fibre_coords, fibre_elem, block_count, fibre_velocity):
    vel = velocity.reshape(3, 128, 512)
    visc = viscosity.reshape(128, 512)
    coords = fibre_coords.reshape(32, 4, 3, 128).transpose(0, 2, 1, 3)
    idents = fibre_elem.reshape(32, 4).transpose(1, 0)
    counts = block_count.reshape(32)
    own_velocity = fibre_velocity.reshape(32, 4, 3, 128).transpose(0, 2, 1, 3)
    (packed,) = call(
        pack_kernel, [(32, 13, 1, 128)], (coords, idents, counts.reshape(1, 32)), specs=[hbm] * 3,
        scratch=[
            pltpu.VMEM((32, 3, 4, 128), f32),
            pltpu.VMEM((4, 32), jnp.int32),
            pltpu.VMEM((1, 32), jnp.int32),
            pltpu.SemaphoreType.DMA((3,)),
        ],
    )
    got = lax.all_to_all(packed, "gz", split_axis=0, concat_axis=0, tiled=True)

    rows = operator_rows()
    field = (3, 128, 512)
    y_face, z_face = (3, 32, 128), (3, 16, 128)
    y_pair, z_pair = (2,) + y_face, (2,) + z_face
    adv, helm, x_sends, y_raw, z_raw, table = call(
        fluid_kernel, [field, field, y_pair, y_pair, z_pair, (48 * 128, 128)], (vel, visc, rows),
        specs=[hbm] * 3,
        out_specs=[hbm] * 2 + [vmem] + [hbm] * 2 + [vmem],
        scratch=[
            pltpu.VMEM((3, 384, 512), f32),
            pltpu.VMEM(y_pair, f32),
            pltpu.VMEM(z_pair, f32),
            pltpu.VMEM(field, f32),
            pltpu.VMEM(field, f32),
            pltpu.VMEM(field, f32),
            pltpu.VMEM((128, 512), f32),
            pltpu.VMEM((56, 128), f32),
            pltpu.VMEM((2, 512, 512), bf16),
            pltpu.VMEM((2, 512, 256), bf16),
            pltpu.SemaphoreType.DMA((14,)),
        ],
    )
    x1, x2 = swap("gx", x_sends[0], x_sends[1])
    got, y_raw = lax.optimization_barrier((got, y_raw))
    (values,) = call(
        fibre_kernel, [(32, 12, 1, 128)], (got, table),
        specs=[vmem, vmem], out_specs=[hbm],
        scratch=[
            pltpu.VMEM((32, 12, 1, 128), f32),
            pltpu.SMEM((128 + 2 * UNROLL,), jnp.int32),
            pltpu.SMEM((32, 128), f32),
            pltpu.SemaphoreType.DMA((2,)),
        ],
    )
    values, x1, x2 = lax.optimization_barrier((values, x1, x2))
    sampled = lax.all_to_all(values, "gz", split_axis=0, concat_axis=0, tiled=True)
    y1, y2, x1, x2, z_raw = call(
        y_face_kernel, [y_face] * 4 + [z_pair], (x1, x2, y_raw, z_raw), specs=[hbm] * 4,
        scratch=[pltpu.VMEM(y_pair, f32), pltpu.SemaphoreType.DMA((4,))],
    )
    y1, y2 = swap("gy", y1, y2)
    z1, z2 = call(
        z_face_kernel, [z_face] * 2, (x1, x2, y1, y2, z_raw), specs=[vmem] * 5,
        scratch=[pltpu.VMEM(z_pair, f32)],
    )
    z1, z2 = swap("gz", z1, z2)
    (work,) = call(
        side_kernel, [(6, 128, 512)], (adv, helm, x1, x2, y1, y2), specs=[hbm, hbm] + [vmem] * 4,
        scratch=[pltpu.SemaphoreType.DMA((6,))],
    )
    adv, helm = call(
        end_kernel, [field, field], (work, z1, z2), specs=[vmem] * 3, out_specs=[hbm] * 2,
        scratch=[pltpu.VMEM((6, 128, 512), f32), pltpu.SemaphoreType.DMA((6,))],
    )
    (drag,) = call(
        drag_kernel, [(32, 3, 4, 128)], (counts, sampled, own_velocity), specs=[smem, vmem, vmem]
    )
    drag = drag.transpose(0, 2, 1, 3).reshape(fibre_coords.shape)
    return adv.reshape(velocity.shape), helm.reshape(velocity.shape), drag


def solution(mesh):
    in_specs = (
        P(None, "gx", "gy", "gz", None),
        P("gx", "gy", "gz", None),
        P("gx", "gy", "gz", None, None, None, None),
        P("gx", "gy", "gz", None, None),
        P("gx", "gy", "gz", None),
        P("gx", "gy", "gz", None, None, None, None),
    )
    out_specs = (
        P(None, "gx", "gy", "gz", None),
        P(None, "gx", "gy", "gz", None),
        P("gx", "gy", "gz", None, None, None, None),
    )
    return jax.shard_map(body, mesh=mesh, in_specs=in_specs, out_specs=out_specs, check_vma=False)
```

```python
import jax
import jax.numpy as jnp
import numpy as np
from jax import lax
from jax.experimental import pallas as pl
from jax.experimental.pallas import tpu as pltpu
from jax.sharding import PartitionSpec as P

gll_points = (
    -1.0,
    -0.8717401485096066,
    -0.5917001814331423,
    -0.2092992179024789,
    0.2092992179024789,
    0.5917001814331423,
    0.8717401485096066,
    1.0,
)
gll_weights = (
    0.03571428571428571,
    0.2107042271435061,
    0.3411226924835044,
    0.4124587946587038,
    0.4124587946587038,
    0.3411226924835044,
    0.2107042271435061,
    0.03571428571428571,
)
helm_shift = 20.0
drag_scale = 0.5
UNROLL = 16
VMEM_LIMIT = 48 * 1024 * 1024
f32 = jnp.float32
bf16 = jnp.bfloat16


def derivative_table():
    points = list(gll_points)
    barycentric = [1.0] * 8
    for row in range(8):
        for other in range(8):
            if other != row:
                barycentric[row] = barycentric[row] / (points[row] - points[other])
    derivative = np.zeros((8, 8))
    for row in range(8):
        total = 0.0
        for other in range(8):
            if other != row:
                entry = barycentric[other] / barycentric[row] / (points[row] - points[other])
                derivative[row, other] = entry
                total = total + entry
        derivative[row, row] = -total
    return derivative


def operator_rows():
    derivative = derivative_table()
    lanes = np.arange(128)
    along_x = np.zeros((8, 4, 128))
    for half in range(2):
        along_x[:, :, 64 * half : 64 * half + 64] = derivative[:, half::2, None]
    along_y = derivative[:, lanes // 8 % 8]
    along_z = derivative[:, lanes % 8]
    rows = np.concatenate([along_x.reshape(32, 128), along_y, along_z]).astype(np.float32)
    weights = np.asarray(gll_weights)
    mass = (weights[:, None, None] * weights[None, :, None] * weights[None, None, :]).reshape(4, 128)
    mass = np.concatenate([mass, np.zeros((4, 128))]).astype(np.float32)
    return np.concatenate([rows, mass])


def fill_operators(rows, dx, dyz):
    row = lax.broadcasted_iota(jnp.int32, (64, 128), 0)
    lane = lax.broadcasted_iota(jnp.int32, (64, 128), 1)
    same = (row & 63) == (lane & 63)
    for a in range(8):
        for tile in range(4):
            values = jnp.where(same, rows[4 * a + tile : 4 * a + tile + 1], 0.0)
            high, low = split(values)
            dx[0, 64 * a : 64 * a + 64, 128 * tile : 128 * tile + 128] = high
            dx[1, 64 * a : 64 * a + 64, 128 * tile : 128 * tile + 128] = low
    row = lax.broadcasted_iota(jnp.int32, (128, 128), 0)
    lane = lax.broadcasted_iota(jnp.int32, (128, 128), 1)
    along_y = jnp.concatenate([jnp.broadcast_to(rows[32 + j % 8 : 33 + j % 8], (8, 128)) for j in range(16)], 0)
    along_z = jnp.concatenate([rows[40:48]] * 16, 0)
    along_y = jnp.where(((row ^ lane) & 71) == 0, along_y, 0.0)
    along_z = jnp.where((row >> 3) == (lane >> 3), along_z, 0.0)
    empty = jnp.zeros((128, 128), bf16)
    for start, values in ((0, along_y), (256, along_z)):
        for n, part in enumerate(split(values)):
            dyz[n, start : start + 128, 0:128] = part
            dyz[n, start : start + 128, 128:256] = empty
            dyz[n, start + 128 : start + 256, 0:128] = empty
            dyz[n, start + 128 : start + 256, 128:256] = part


def pick_table(face):
    node = lax.broadcasted_iota(jnp.int32, (512, 128), 0)
    lane = lax.broadcasted_iota(jnp.int32, (512, 128), 1)
    i, j, k = node >> 6, (node >> 3) & 7, node & 7
    edge = 7 * (face % 2)
    if face < 2:
        hit = (j == edge) & (lane == i * 8 + k)
    else:
        hit = (k == edge) & (lane == i * 8 + j)
    return jnp.where(hit, 1.0, 0.0).astype(bf16)


def edge_table(side, place):
    source = lax.broadcasted_iota(jnp.int32, (128, 128), 0)
    lane = lax.broadcasted_iota(jnp.int32, (128, 128), 1)
    target = (source & 64) + 56 * place + ((source >> 3) & 7)
    hit = ((source & 7) == 7 * side) & (lane == target)
    return jnp.where(hit, 1.0, 0.0).astype(bf16)


def basis_rows():
    node = lax.broadcasted_iota(jnp.int32, (8, 128), 0)
    rows = []
    for place in range(7):
        value = jnp.full((8, 128), gll_points[place + 1], f32)
        for row in range(place + 1, 8):
            value = jnp.where(node == row, gll_points[place], value)
        rows.append(value)
    scales = jnp.ones((8, 128), f32)
    for row in range(8):
        scale = 1.0
        for other in range(8):
            if other != row:
                scale = scale / (gll_points[row] - gll_points[other])
        scales = jnp.where(node == row, scale, scales)
    return rows, scales


def split(x):
    high = x.astype(bf16)
    low = (x - high.astype(f32)).astype(bf16)
    return high, low


def mm(a, b, dims=((1,), (0,))):
    return lax.dot_general(a, b, (dims, ((), ())), preferred_element_type=f32)


def dot3(x, table, side):
    high, low = split(x)
    dims = ((1,), (side,))
    return mm(high, table[0], dims) + mm(high, table[1], dims) + mm(low, table[0], dims)


def pick(x, table):
    high, low = split(x)
    return mm(high, table) + mm(low, table)


def pick_both(first, second, table):
    rows = first.shape[0]
    got = mm(jnp.concatenate(split(first) + split(second), 0), table)
    one = got[0:rows] + got[rows : 2 * rows]
    two = got[2 * rows : 3 * rows] + got[3 * rows :]
    return one + pltpu.roll(two, 64, 1)


def spread(x, table):
    high, low = split(x)
    dims = ((1,), (1,))
    return mm(high, table, dims) + mm(low, table, dims)


def lane_iota(shape):
    return lax.broadcasted_iota(jnp.int32, shape, len(shape) - 1)


def fluid_kernel(vel_in, visc_in, rows_in, adv_out, helm_out, x_work, y_out, z_out, table, flux, y_work, z_work, adv, helm, vel, visc, rows, dx, dyz, sems):
    pairs = ((rows_in, rows), (vel_in, vel), (visc_in, visc))
    loads = [pltpu.make_async_copy(a, b, sems.at[n]) for n, (a, b) in enumerate(pairs)]
    for load in loads:
        load.start()
    loads[0].wait()
    fill_operators(rows, dx, dyz)
    loads[1].wait()
    v = vel[...].reshape(384, 512)
    flux[0] = dot3(v, dx, 1)
    for half in range(2):
        lanes = slice(256 * half, 256 * half + 256)
        g = dot3(v[:, lanes], dyz, 1)
        flux[1, :, lanes] = g[:, :256]
        flux[2, :, lanes] = g[:, 256:]
    loads[2].wait()
    mass = jnp.concatenate([rows[48 + tile : 49 + tile] for tile in range(4)], 1)
    weighted = mass * visc[...]
    for c in range(3):
        rows = slice(128 * c, 128 * c + 128)
        total = vel[0] * flux[0, rows] + vel[1] * flux[1, rows] + vel[2] * flux[2, rows]
        adv[c] = mass * total
        for d in range(3):
            flux[d, rows] = weighted * flux[d, rows]
    stiff = dot3(flux[0], dx, 0)
    helm[...] = (stiff + (helm_shift * mass) * v).reshape(3, 128, 512)
    for half in range(2):
        lanes = slice(256 * half, 256 * half + 256)
        both = jnp.concatenate([flux[1, :, lanes], flux[2, :, lanes]], axis=1)
        helm[:, :, lanes] = helm[:, :, lanes] + dot3(both, dyz, 0).reshape(3, 128, 256)
    stores = []
    for field, out in ((adv, adv_out), (helm, helm_out)):
        for c in range(3):
            local_sums(field, c)
            stores.append(pltpu.make_async_copy(field.at[c], out.at[c], sems.at[5 + len(stores)]))
            stores[-1].start()
    lane = lane_iota((32, 128))
    odd = lax.axis_index("gx") % 2
    for c in range(3):
        left = jnp.where(lane < 64, adv[c, 0:32, 0:128], pltpu.roll(helm[c, 0:32, 0:128], 64, 1))
        right = jnp.where(lane < 64, pltpu.roll(adv[c, 96:128, 384:512], 64, 1), helm[c, 96:128, 384:512])
        x_work[1 - odd, c] = left
        x_work[odd, c] = right
    for out, start, side in ((y_work.at[0], 0, 0), (y_work.at[1], 24, 1)):
        faces = [field[...].reshape(12, 32, 512)[:, start : start + 8].reshape(96, 512) for field in (adv, helm)]
        out[...] = pick_both(*faces, pick_table(side)).reshape(3, 32, 128)
    for out, start, side in ((z_work.at[0], 0, 2), (z_work.at[1], 7, 3)):
        faces = [field[...].reshape(48, 8, 512)[:, start] for field in (adv, helm)]
        out[...] = pick_both(*faces, pick_table(side)).reshape(3, 16, 128)
    stores.append(pltpu.make_async_copy(y_work, y_out, sems.at[12]))
    stores[-1].start()
    stores.append(pltpu.make_async_copy(z_work, z_out, sems.at[13]))
    stores[-1].start()
    fill_table(vel, table, range(4))
    for store in stores:
        store.wait()


def local_sums(field, c):
    lane = lane_iota((96, 128))
    upper = field[c, 0:96, 384:512]
    lower = field[c, 32:128, 0:128]
    field[c, 0:96, 384:512] = upper + jnp.where(lane >= 64, pltpu.roll(lower, 64, 1), 0.0)
    field[c, 32:128, 0:128] = lower + jnp.where(lane < 64, pltpu.roll(upper, 64, 1), 0.0)
    for tile in range(4):
        lanes = slice(128 * tile, 128 * tile + 128)
        y = field[c, :, lanes].reshape(4, 32, 128)
        below = y[:, 0:24].reshape(96, 128)
        above = y[:, 8:32].reshape(96, 128)
        j = lane // 8 % 8
        to_below = jnp.where(j == 7, pltpu.roll(above, 56, 1), 0.0).reshape(4, 24, 128)
        to_above = jnp.where(j == 0, pltpu.roll(below, 72, 1), 0.0).reshape(4, 24, 128)
        gap = jnp.zeros((4, 8, 128), f32)
        y = y + jnp.concatenate([to_below, gap], 1) + jnp.concatenate([gap, to_above], 1)
        z = y.reshape(16, 8, 128)
        lane_z = lane_iota((16, 8, 128)) % 8
        level = lax.broadcasted_iota(jnp.int32, (16, 8, 128), 1)
        from_below = pltpu.roll(pltpu.roll(z, 121, 2), 1, 1)
        from_above = pltpu.roll(pltpu.roll(z, 7, 2), 7, 1)
        z = z + jnp.where((lane_z == 0) & (level > 0), from_below, 0.0)
        z = z + jnp.where((lane_z == 7) & (level < 7), from_above, 0.0)
        field[c, :, lanes] = z.reshape(128, 128)


def both_sides(odd, first, second):
    flag = jnp.full((8, 128), odd, jnp.int32) == 1

    def below(c, rows):
        flags = flag[: rows.stop - rows.start]
        return jnp.where(flags, first[c, rows], second[c, rows])

    def above(c, rows):
        flags = flag[: rows.stop - rows.start]
        return jnp.where(flags, second[c, rows], first[c, rows])

    return below, above


def y_face_kernel(x1_in, x2_in, y_in, z_in, y1, y2, x1, x2, z, y_raw, sems):
    pairs = ((x1_in, x1), (x2_in, x2), (y_in, y_raw), (z_in, z))
    loads = [pltpu.make_async_copy(a, b, sems.at[n]) for n, (a, b) in enumerate(pairs)]
    for load in loads:
        load.start()
    for load in loads:
        load.wait()
    lane = lane_iota((8, 128)) % 64
    xb, xa = both_sides(lax.axis_index("gx") % 2, x1, x2)
    odd = jnp.full((8, 128), lax.axis_index("gy") % 2, jnp.int32) == 1
    head, tail = slice(0, 8), slice(24, 32)
    for c in range(3):
        extra = {
            (0, 0): jnp.where(lane < 8, xb(c, head), 0.0),
            (1, 0): jnp.where(lane < 8, pltpu.roll(xb(c, tail), 72, 1), 0.0),
            (0, 3): jnp.where(lane >= 56, pltpu.roll(xa(c, head), 56, 1), 0.0),
            (1, 3): jnp.where(lane >= 56, xa(c, tail), 0.0),
        }
        for a in range(4):
            rows = slice(8 * a, 8 * a + 8)
            left, right = y_raw[0, c, rows], y_raw[1, c, rows]
            if a in (0, 3):
                left = left + extra[0, a]
                right = right + extra[1, a]
            y1[c, rows] = jnp.where(odd, left, right)
            y2[c, rows] = jnp.where(odd, right, left)


def z_face_kernel(x1, x2, y1, y2, z_raw, out1, out2, z):
    z[...] = z_raw[...]
    lane = lane_iota((1, 128)) % 8
    x_odd = jnp.full((96, 128), lax.axis_index("gx") % 2, jnp.int32) == 1
    x_first, x_second = x1[...].reshape(96, 128), x2[...].reshape(96, 128)
    xb, xa = jnp.where(x_odd, x_first, x_second), jnp.where(x_odd, x_second, x_first)
    yb, ya = both_sides(lax.axis_index("gy") % 2, y1, y2)
    for level, side in ((0, 0), (7, 1)):
        for got, place in ((xb, 0), (xa, 1)):
            part = pick(got, edge_table(side, place))
            for c in range(3):
                for b in range(4):
                    source = 32 * c + 8 * b + level
                    row = 12 * place + b
                    z[side, c, row : row + 1] += part[source : source + 1]
        for c in range(3):
            for a in range(4):
                row = slice(8 * a + level, 8 * a + level + 1)
                below, above = yb(c, row), ya(c, row)
                if side:
                    below = pltpu.roll(below, 121, 1)
                else:
                    above = pltpu.roll(above, 7, 1)
                z[side, c, 4 * a : 4 * a + 1] += jnp.where(lane == 0, below, 0.0)
                z[side, c, 4 * a + 3 : 4 * a + 4] += jnp.where(lane == 7, above, 0.0)
    odd = jnp.full((3, 16, 128), lax.axis_index("gz") % 2, jnp.int32) == 1
    out1[...] = jnp.where(odd, z[0], z[1])
    out2[...] = jnp.where(odd, z[1], z[0])


def sides(odd, first, second):
    rows = first.shape[0] * first.shape[1]
    flag = jnp.full((rows, 128), odd, jnp.int32) == 1
    one, two = first[...].reshape(rows, 128), second[...].reshape(rows, 128)
    below, above = jnp.where(flag, one, two), jnp.where(flag, two, one)
    return [[got, pltpu.roll(got, 64, 1)] for got in (below, above)]


def side_kernel(adv_in, helm_in, x1, x2, y1, y2, work, sems):
    loads = []
    for c in range(3):
        for part, source in enumerate((adv_in, helm_in)):
            n = 3 * part + c
            loads.append(pltpu.make_async_copy(source.at[c], work.at[n], sems.at[n]))
            loads[-1].start()
    lane = lane_iota((32, 128))
    x_sides = sides(lax.axis_index("gx") % 2, x1, x2)
    y_sides = sides(lax.axis_index("gy") % 2, y1, y2)
    wide = [[spread(y_sides[side][part], pick_table(side)) for side in range(2)] for part in range(2)]
    for load in loads:
        load.wait()
    for part in range(2):
        for c in range(3):
            n = 3 * part + c
            faces = slice(32 * c, 32 * c + 32)
            work[n, 0:32, 0:128] += jnp.where(lane < 64, x_sides[0][part][faces], 0.0)
            work[n, 96:128, 384:512] += jnp.where(lane >= 64, x_sides[1][1 - part][faces], 0.0)
            for side, start in ((0, 0), (1, 24)):
                for a in range(4):
                    row = 32 * a + start
                    source = 32 * c + 8 * a
                    work[n, row : row + 8] += wide[part][side][source : source + 8]


def end_kernel(work, z1, z2, adv, helm, done, sems):
    level = lax.broadcasted_iota(jnp.int32, (16, 8, 512), 1)
    z_sides = sides(lax.axis_index("gz") % 2, z1, z2)
    stores = []
    for part, target in enumerate((adv, helm)):
        ends = [spread(z_sides[side][part], pick_table(2 + side)) for side in range(2)]
        for c in range(3):
            n = 3 * part + c
            rows = slice(16 * c, 16 * c + 16)
            total = work[n].reshape(16, 8, 512)
            total = total + jnp.where(level == 0, ends[0][rows][:, None, :], 0.0)
            total = total + jnp.where(level == 7, ends[1][rows][:, None, :], 0.0)
            done[n] = total.reshape(128, 512)
            stores.append(pltpu.make_async_copy(done.at[n], target.at[c], sems.at[n]))
            stores[-1].start()
    for store in stores:
        store.wait()


def drag_kernel(counts, sampled, own, out):
    slot = lax.broadcasted_iota(jnp.int32, (4, 128), 0)
    for source in range(32):
        relative = [sampled[source, 4 * d : 4 * d + 4, 0] - own[source, d] for d in range(3)]
        square = relative[0] * relative[0] + relative[1] * relative[1] + relative[2] * relative[2]
        factor = jnp.where(slot < counts[source], drag_scale * jnp.sqrt(1.0 + square), 0.0)
        for d in range(3):
            out[source, d] = jnp.where(slot < counts[source], factor * relative[d], 0.0)


def pack_kernel(coords_in, idents_in, counts_in, out_hbm, coords, idents, counts, out, sems):
    pairs = [(idents_in, idents), (counts_in, counts)]
    for part in range(4):
        rows = pl.ds(8 * part, 8)
        pairs.append((coords_in.at[rows], coords.at[rows]))
    loads = [pltpu.make_async_copy(a, b, sems.at[n]) for n, (a, b) in enumerate(pairs)]
    for load in loads:
        load.start()
    loads[0].wait()
    loads[1].wait()
    slot = lax.broadcasted_iota(jnp.int32, (4, 32), 0)
    tags = jnp.where(slot < counts[...], idents[...], -1).astype(f32)
    tags = jnp.concatenate([tags[q : q + 1] for q in range(4)], axis=1)
    stores = []
    for part in range(4):
        loads[2 + part].wait()
        for source in range(8 * part, 8 * part + 8):
            for d in range(3):
                out[source, 4 * d : 4 * d + 4, 0] = coords[source, d]
            out[source, 12] = tags
        rows = pl.ds(8 * part, 8)
        stores.append(pltpu.make_async_copy(out.at[rows], out_hbm.at[rows], sems.at[6 + part]))
        stores[-1].start()
    for store in stores:
        store.wait()


def fill_table(vel, table, tiles):
    lane = lane_iota((128, 128))
    for c in range(3):
        for tile in tiles:
            x = vel[c, :, 128 * tile : 128 * tile + 128]
            high = x.astype(bf16).astype(f32)
            low = x - high
            for part in range(4):
                i, j_high = 2 * tile + part // 2, part % 2
                shift = -32 * part
                a = pltpu.roll(high, shift % 128, 1) if part else high
                b = pltpu.roll(low, (shift + 32) % 128, 1) if (shift + 32) % 128 else low
                d = pltpu.roll(high, (shift + 64) % 128, 1) if (shift + 64) % 128 else high
                row = (j_high * 3 + c) * 8 + i
                mixed = jnp.where(lane < 32, a, jnp.where(lane < 64, b, jnp.where(lane < 96, d, 0.0)))
                table[128 * row : 128 * row + 128] = mixed


def fibre_kernel(got, table, out_hbm, out, live, tags, sems):
    load_tags = pltpu.make_async_copy(got.at[:, 12, 0], tags, sems.at[0])
    load_tags.start()
    load_tags.wait()
    me = lax.axis_index("gz")

    def ids(block):
        return tags[block // 4, block % 4 * 32 + me]

    for slot in range(128 + UNROLL):
        live[slot] = 0

    def gather(block, count):
        live[count] = block
        return count + jnp.where(ids(block) >= 0.0, 1, 0)

    count = lax.fori_loop(0, 128, gather, 0, unroll=8)
    live[count] = 0
    rows, scales = basis_rows()

    def weights(position):
        value = scales
        for row in rows:
            value = value * (position - row)
        return value

    def one(block):
        source = block // 4
        slot = block % 4
        elem = jnp.maximum(ids(block), 0.0).astype(jnp.int32)
        nodes = table[pl.ds(elem, 48, stride=128), :].astype(bf16)
        basis_x, basis_y, basis_z = (
            weights(jnp.broadcast_to(got[source, 4 * d + slot], (8, 128))) for d in range(3)
        )
        high = basis_z.astype(bf16).astype(f32)
        low = basis_z - high
        zero = jnp.zeros((8, 128), f32)
        empty = jnp.zeros((16, 128), bf16)
        highs = [jnp.concatenate(pair, 0).astype(bf16) for pair in ((high, zero), (zero, high))]
        lows = [jnp.concatenate(pair, 0).astype(bf16) for pair in ((low, zero), (zero, low))]
        columns = []
        for j in range(4):
            pieces = [empty] * 8
            pieces[j // 2] = highs[j % 2]
            pieces[2 + j // 2] = highs[j % 2]
            pieces[4 + j // 2] = lows[j % 2]
            columns.append(jnp.concatenate(pieces, 0))
        sections = [mm(nodes, column) for column in columns]
        for c in range(3):
            total = jnp.zeros((8, 128), f32)
            for j in range(8):
                top = (j // 4 * 3 + c) * 8
                total = total + sections[j % 4][top : top + 8] * basis_y[j : j + 1]
            out[source, 4 * c + slot] = jnp.sum(total * basis_x, axis=0, keepdims=True)

    def group(step, carry):
        for u in range(UNROLL):
            one(live[step * UNROLL + u])
        return carry

    lax.fori_loop(0, (count + UNROLL - 1) // UNROLL, group, 0)
    store = pltpu.make_async_copy(out, out_hbm, sems.at[1])
    store.start()
    store.wait()


vmem = pl.BlockSpec(memory_space=pltpu.VMEM)
hbm = pl.BlockSpec(memory_space=pltpu.HBM)
smem = pl.BlockSpec(memory_space=pltpu.SMEM)


def call(kernel, outs, args, specs=None, scratch=(), out_specs=None):
    out_specs = out_specs or [vmem] * len(outs)
    args = [
        pltpu.with_memory_space_constraint(arg, pltpu.HBM) if spec is hbm else arg
        for arg, spec in zip(args, specs or [vmem] * len(args))
    ]
    shapes = [
        pltpu.HBM(shape, f32) if spec is hbm else jax.ShapeDtypeStruct(shape, f32)
        for shape, spec in zip(outs, out_specs)
    ]
    return pl.pallas_call(
        kernel,
        out_shape=shapes,
        in_specs=specs or [vmem] * len(args),
        out_specs=out_specs,
        scratch_shapes=list(scratch),
        compiler_params=pltpu.CompilerParams(vmem_limit_bytes=VMEM_LIMIT),
        name=kernel.__name__,
    )(*args)


def swap(axis, first, second):
    size = lax.axis_size(axis)
    even_pairs = [(i, i ^ 1) for i in range(size)]
    odd_pairs = [(i, ((i + 1) ^ 1) - 1) for i in range(1, size - 1)]
    return lax.ppermute(first, axis, even_pairs), lax.ppermute(second, axis, odd_pairs)


def body(velocity, viscosity, fibre_coords, fibre_elem, block_count, fibre_velocity):
    vel = velocity.reshape(3, 128, 512)
    visc = viscosity.reshape(128, 512)
    coords = fibre_coords.reshape(32, 4, 3, 128).transpose(0, 2, 1, 3)
    idents = fibre_elem.reshape(32, 4).transpose(1, 0)
    counts = block_count.reshape(32)
    own_velocity = fibre_velocity.reshape(32, 4, 3, 128).transpose(0, 2, 1, 3)
    (packed,) = call(
        pack_kernel, [(32, 13, 1, 128)], (coords, idents, counts.reshape(1, 32)), specs=[hbm] * 3, out_specs=[hbm],
        scratch=[
            pltpu.VMEM((32, 3, 4, 128), f32),
            pltpu.VMEM((4, 32), jnp.int32),
            pltpu.VMEM((1, 32), jnp.int32),
            pltpu.VMEM((32, 13, 1, 128), f32),
            pltpu.SemaphoreType.DMA((10,)),
        ],
    )
    got = lax.all_to_all(packed, "gz", split_axis=0, concat_axis=0, tiled=True)

    rows = operator_rows()
    field = (3, 128, 512)
    y_face, z_face = (3, 32, 128), (3, 16, 128)
    y_pair, z_pair = (2,) + y_face, (2,) + z_face
    adv, helm, x_sends, y_raw, z_raw, table = call(
        fluid_kernel, [field, field, y_pair, y_pair, z_pair, (48 * 128, 128)], (vel, visc, rows),
        specs=[hbm] * 3,
        out_specs=[hbm] * 2 + [vmem] + [hbm] * 2 + [vmem],
        scratch=[
            pltpu.VMEM((3, 384, 512), f32),
            pltpu.VMEM(y_pair, f32),
            pltpu.VMEM(z_pair, f32),
            pltpu.VMEM(field, f32),
            pltpu.VMEM(field, f32),
            pltpu.VMEM(field, f32),
            pltpu.VMEM((128, 512), f32),
            pltpu.VMEM((56, 128), f32),
            pltpu.VMEM((2, 512, 512), bf16),
            pltpu.VMEM((2, 512, 256), bf16),
            pltpu.SemaphoreType.DMA((14,)),
        ],
    )
    x1, x2 = swap("gx", x_sends[0], x_sends[1])
    got, y_raw = lax.optimization_barrier((got, y_raw))
    (values,) = call(
        fibre_kernel, [(32, 12, 1, 128)], (got, table),
        specs=[vmem, vmem], out_specs=[hbm],
        scratch=[
            pltpu.VMEM((32, 12, 1, 128), f32),
            pltpu.SMEM((128 + 2 * UNROLL,), jnp.int32),
            pltpu.SMEM((32, 128), f32),
            pltpu.SemaphoreType.DMA((2,)),
        ],
    )
    values, x1, x2 = lax.optimization_barrier((values, x1, x2))
    sampled = lax.all_to_all(values, "gz", split_axis=0, concat_axis=0, tiled=True)
    y1, y2, x1, x2, z_raw = call(
        y_face_kernel, [y_face] * 4 + [z_pair], (x1, x2, y_raw, z_raw), specs=[hbm] * 4,
        scratch=[pltpu.VMEM(y_pair, f32), pltpu.SemaphoreType.DMA((4,))],
    )
    y1, y2 = swap("gy", y1, y2)
    z1, z2 = call(
        z_face_kernel, [z_face] * 2, (x1, x2, y1, y2, z_raw), specs=[vmem] * 5,
        scratch=[pltpu.VMEM(z_pair, f32)],
    )
    z1, z2 = swap("gz", z1, z2)
    (work,) = call(
        side_kernel, [(6, 128, 512)], (adv, helm, x1, x2, y1, y2), specs=[hbm, hbm] + [vmem] * 4,
        scratch=[pltpu.SemaphoreType.DMA((6,))],
    )
    adv, helm = call(
        end_kernel, [field, field], (work, z1, z2), specs=[vmem] * 3, out_specs=[hbm] * 2,
        scratch=[pltpu.VMEM((6, 128, 512), f32), pltpu.SemaphoreType.DMA((6,))],
    )
    (drag,) = call(
        drag_kernel, [(32, 3, 4, 128)], (counts, sampled, own_velocity), specs=[smem, vmem, vmem]
    )
    drag = drag.transpose(0, 2, 1, 3).reshape(fibre_coords.shape)
    return adv.reshape(velocity.shape), helm.reshape(velocity.shape), drag


def solution(mesh):
    in_specs = (
        P(None, "gx", "gy", "gz", None),
        P("gx", "gy", "gz", None),
        P("gx", "gy", "gz", None, None, None, None),
        P("gx", "gy", "gz", None, None),
        P("gx", "gy", "gz", None),
        P("gx", "gy", "gz", None, None, None, None),
    )
    out_specs = (
        P(None, "gx", "gy", "gz", None),
        P(None, "gx", "gy", "gz", None),
        P("gx", "gy", "gz", None, None, None, None),
    )
    return jax.shard_map(body, mesh=mesh, in_specs=in_specs, out_specs=out_specs, check_vma=False)
```
